128 devices in a mesh: row: 8 (over y_hi, z), col: 8 (over x, y_lo), depth: 2 (over core).
Axes of the slice: x: 4, y: 4 (y_hi: 2, y_lo: 2; y = y_hi * 2 + y_lo), z: 4, core: 2. Of those that a mesh axis runs over, the one named last changes fastest.
Arguments:
- lambdas: float32 [3200, 11264], P(('col', 'depth'), 'row'), may hold values from -0.109375 to 0.109375
- amplitudes: float32 [3200, 11264], P(('row', 'depth'), 'col'), may hold values from -6 to 6
- virt_irrep: int32 [1200], replicated, may hold values from 0 to 7
- ab_first: int32 [11264], P(('row', 'depth')), may hold values from 0 to 1199
- ab_second: int32 [11264], P(('row', 'depth')), may hold values from 0 to 1199
- cd_first: int32 [11264], P('col'), may hold values from 0 to 1199
- cd_second: int32 [11264], P('col'), may hold values from 0 to 1199
Outputs:
- density_tile: float32 [11264, 11264], P(('row', 'depth'), 'col')
The draws below stay inside these ranges and needn't reach their ends.
Inputs may be any that keep to these rules, and one draw needn't show every extreme that they name: `virt_irrep`: irrep labels of the eight D2h irreps. `ab_first`: indices of virtual orbitals. `ab_second`: indices of virtual orbitals. `cd_first`: indices of virtual orbitals. `cd_second`: indices of virtual orbitals.
All inputs are finite; a program needn't handle non-finite values.
Results may differ from the reference program's by a relative error of at most 0.00007.
Values sent between devices are 32-bit elements; how exact they have to be, the bound alone decides.
A program may use at most 128 MiB of HBM per device.

```python
import jax
import jax.numpy as jnp
from jax import lax

AB = 11264
CD = 11264
NVIRT = 1200
PAIRS = 3200


def place_ends(array, own_key, smallest, top_value):
    index_at = [jax.random.randint(jax.random.fold_in(own_key, axis), (), 0, length) for axis, length in enumerate(array.shape)]
    widest = array.shape.index(max(array.shape))
    next_to = index_at[:widest] + [(index_at[widest] + 1) % array.shape[widest]] + index_at[widest + 1:]
    return array.at[tuple(index_at)].set(smallest).at[tuple(next_to)].set(top_value)


def shard_levels(stream_key, shape, split, smallest, largest):
    factor_of, own = 1.0, jax.random.fold_in(stream_key, 6)
    for axis_at, shards_of in split:
        heights = jnp.exp(jax.random.uniform(jax.random.fold_in(own, axis_at), (shards_of,), jnp.float32, smallest / len(split), largest / len(split)))
        factor_of = factor_of * jnp.repeat(heights, shape[axis_at] // shards_of).reshape([-1 if axis == axis_at else 1 for axis in range(len(shape))])
    return factor_of


def normal_values(rng, extent, spread, reach, cuts=(), held_as=jnp.bfloat16):
    loudness = shard_levels(rng, extent, cuts, -0.22, 0.18) if cuts else 1.0
    drawn = jax.random.normal(rng, extent, jnp.float32) * spread * loudness
    return jnp.minimum(jnp.maximum(drawn, -reach), reach).astype(held_as)


def setup_inputs(seed: int = 0) -> dict:
    splits = jax.random.split(jax.random.key(seed), 8)
    return {
        "lambdas": normal_values(splits[0], (PAIRS, AB), PAIRS ** -0.5, 0.109375, ((0, 16), (1, 8)), jnp.float32),
        "amplitudes": normal_values(splits[1], (PAIRS, CD), 1.0, 6.0, ((0, 16), (1, 8)), jnp.float32),
        "virt_irrep": place_ends(jax.random.randint(splits[2], (NVIRT,), 0, 8), jax.random.fold_in(splits[2], 1), 0, 7).astype(jnp.int32),
        "ab_first": place_ends(jax.random.randint(splits[3], (AB,), 0, NVIRT), jax.random.fold_in(splits[3], 1), 0, NVIRT - 1).astype(jnp.int32),
        "ab_second": place_ends(jax.random.randint(splits[4], (AB,), 0, NVIRT), jax.random.fold_in(splits[4], 1), 0, NVIRT - 1).astype(jnp.int32),
        "cd_first": place_ends(jax.random.randint(splits[5], (CD,), 0, NVIRT), jax.random.fold_in(splits[5], 1), 0, NVIRT - 1).astype(jnp.int32),
        "cd_second": place_ends(jax.random.randint(splits[6], (CD,), 0, NVIRT), jax.random.fold_in(splits[6], 1), 0, NVIRT - 1).astype(jnp.int32),
    }


def pair_signs(first, second, virt_irrep):
    return jnp.where(virt_irrep[first] > virt_irrep[second], -1.0, 1.0).astype(jnp.float32)


def reference(lambdas, amplitudes, virt_irrep, ab_first, ab_second, cd_first, cd_second):
    gamma_sum = lax.dot_general(lambdas, amplitudes, (((0,), (0,)), ((), ())), precision=lax.Precision.HIGHEST, preferred_element_type=jnp.float32)
    sign_ab = pair_signs(ab_first, ab_second, virt_irrep)
    sign_cd = pair_signs(cd_first, cd_second, virt_irrep)
    return gamma_sum * sign_ab[:, None] * sign_cd[None, :]
```

```python
import functools

import jax
import jax.numpy as jnp
from jax import lax
from jax.experimental import pallas as pl
from jax.experimental.pallas import tpu as pltpu
from jax.sharding import PartitionSpec as P

MESH = pl.DeviceIdType.MESH
F32, BF16 = jnp.float32, jnp.bfloat16

CHUNKS, ROWS = 11, 16
LAST_ROWS = 24
LAST_AT = (0, 2, 5, 7)
SOURCES = 8
WIDTH = 1408
HALF = 704
HALF_LANES = 768
HALF_AT = 640


class Side:
    def __init__(self, own, buf, last, me, ring, plane, device, send, recv, last_send, last_recv, core):
        self.own, self.buf, self.last = own, buf, last
        self.me, self.ring, self.plane, self.device = me, ring, plane, device
        self.send, self.recv, self.last_send, self.last_recv = send, recv, last_send, last_recv
        self.core, self.way = core, 1 - 2 * core

    def rows(self, block):
        at = self.core * (SOURCES * ROWS) + block * ROWS
        return pl.ds(pl.multiple_of(at, ROWS), ROWS)

    def last_rows(self, block):
        at = self.core * (SOURCES * LAST_ROWS) + block * LAST_ROWS
        return pl.ds(pl.multiple_of(at, 8), LAST_ROWS)

    def put(self, j, block, target, kind, own=False):
        here = self.buf.at[j, self.rows(block)]
        src = self.own.at[pl.ds(pl.multiple_of(j * ROWS, ROWS), ROWS)] if own else here
        pltpu.make_async_remote_copy(
            src_ref=src,
            dst_ref=here,
            send_sem=self.send.at[j],
            recv_sem=self.recv.at[j, kind],
            device_id=self.device(target),
            device_id_type=MESH,
        ).start()

    def got(self, j, kind, count=1):
        part = self.buf.at[j, pl.ds(0, count * ROWS)]
        pltpu.make_async_copy(part, part, self.recv.at[j, kind]).wait()

    def sent(self, j):
        part = self.buf.at[j, pl.ds(0, 7 * ROWS)]
        pltpu.make_async_copy(part, part, self.send.at[j]).wait()

    def cross_own(self, j):
        self.put(j, self.me, self.plane(self.me), 0, own=True)

    def ring_own(self, j):
        self.put(j, self.me, self.ring(self.me, self.way), 1, own=True)
        self.put(j, self.me, self.ring(self.me, -self.way), 3, own=True)

    def ring_partner(self, j):
        self.got(j, 0)
        block = self.plane(self.me)
        self.put(j, block, self.ring(self.me, self.way), 2)
        self.put(j, block, self.ring(self.me, -self.way), 3)

    def pass_own(self, j):
        self.got(j, 1)
        self.put(j, self.ring(self.me, -self.way), self.ring(self.me, self.way), 3)

    def pass_partner(self, j):
        self.got(j, 2)
        block = self.plane(self.ring(self.me, -self.way))
        self.put(j, block, self.ring(self.me, self.way), 3)

    def put_last(self, block, target, kind, own=False):
        here = self.last.at[self.last_rows(block)]
        src = self.own.at[pl.ds(CHUNKS * ROWS, LAST_ROWS)] if own else here
        pltpu.make_async_remote_copy(
            src_ref=src,
            dst_ref=here,
            send_sem=self.last_send,
            recv_sem=self.last_recv.at[kind],
            device_id=self.device(target),
            device_id_type=MESH,
        ).start()

    def got_last(self, kind):
        part = self.last.at[pl.ds(0, LAST_ROWS)]
        pltpu.make_async_copy(part, part, self.last_recv.at[kind]).wait()

    def sent_last(self):
        part = self.last.at[pl.ds(0, 7 * LAST_ROWS)]
        pltpu.make_async_copy(part, part, self.last_send).wait()

    def ring_last(self):
        self.put_last(self.me, self.ring(self.me, self.way), 0, own=True)
        self.put_last(self.me, self.ring(self.me, -self.way), 1, own=True)

    def pass_last(self):
        self.got_last(0)
        self.put_last(self.ring(self.me, -self.way), self.ring(self.me, self.way), 2)

    def cross_last(self, step):
        if step >= 2:
            self.got_last(step - 1)
        offset = (0, -self.way, self.way, 2)[step]
        self.put_last(self.ring(self.me, offset), self.plane(self.me), 3 + step)


def kernel(
    lam, amp, out,
    lam_buf, amp_buf, lam_last, amp_last, left, right,
    local_sem, lam_send, amp_send, lam_recv, amp_recv, lam_last_send, amp_last_send, lam_last_recv, amp_last_recv,
    core_send, core_recv, core_last_send, core_last_recv,
):
    row, col, core = lax.axis_index("row"), lax.axis_index("col"), lax.axis_index("depth")

    lam_side = Side(
        lam, lam_buf, lam_last, col,
        lambda k, s: (k + 2 * s + 8) % 8,
        lambda k: k + 1 - 2 * (k % 2),
        lambda k: (row, k, core),
        lam_send, lam_recv, lam_last_send, lam_last_recv, core,
    )
    amp_side = Side(
        amp, amp_buf, amp_last, row,
        lambda k, s: k // 4 * 4 + (k + s + 4) % 4,
        lambda k: (k + 4) % 8,
        lambda k: (k, col, core),
        amp_send, amp_recv, amp_last_send, amp_last_recv, core,
    )
    sides = (lam_side, amp_side)
    other = (row, col, 1 - core)

    barrier = pltpu.get_barrier_semaphore()
    partners = [other]
    for side in sides:
        partners += [side.device(k) for k in (side.plane(side.me), side.ring(side.me, 1), side.ring(side.me, -1))]
    for partner in partners:
        pl.semaphore_signal(barrier, inc=1, device_id=partner, device_id_type=MESH)
    pl.semaphore_wait(barrier, len(partners))

    for side in sides:
        side.cross_own(0)
    for side in sides:
        side.ring_own(0)
    for side in sides:
        side.ring_last()
    for side in sides:
        side.cross_own(1)

    def lay(j, _):
        for i, side in enumerate(sides):
            src = side.own.at[pl.ds(pl.multiple_of(j * ROWS, ROWS), ROWS)]
            pltpu.make_async_copy(src, side.buf.at[j, side.rows(side.me)], local_sem.at[i]).start()
        return 0

    lax.fori_loop(0, CHUNKS, lay, 0)
    for i, side in enumerate(sides):
        src = side.own.at[pl.ds(CHUNKS * ROWS, LAST_ROWS)]
        pltpu.make_async_copy(src, side.last.at[side.last_rows(side.me)], local_sem.at[i]).start()
    out[...] = jnp.zeros_like(out)
    for i, side in enumerate(sides):
        pltpu.make_async_copy(side.own, side.own, local_sem.at[i]).wait()

    def lanes(of):
        return pl.ds(pl.multiple_of(HALF_AT * of, 128), HALF_LANES)

    def core_copies(lam_rows, amp_rows, send, recv):
        lam_part = lam_rows.at[:, lanes(1 - core)]
        return [
            pltpu.make_async_remote_copy(
                src_ref=part, dst_ref=part, send_sem=send.at[i], recv_sem=recv.at[i], device_id=other, device_id_type=MESH
            )
            for i, part in enumerate((lam_part, amp_rows))
        ]

    def share(j):
        mine = pl.ds(pl.multiple_of(core * (SOURCES * ROWS), 128), SOURCES * ROWS)
        return core_copies(lam_buf.at[j, mine], amp_buf.at[j, mine], core_send.at[j], core_recv.at[j])

    def share_last():
        mine = pl.ds(pl.multiple_of(core * (SOURCES * LAST_ROWS), 64), SOURCES * LAST_ROWS)
        return core_copies(lam_last.at[mine], amp_last.at[mine], core_last_send, core_last_recv)

    def multiply(lam_rows, amp_rows):
        depth = lam_rows.shape[0]
        l = lam_rows[:, lanes(core)].T
        l_hi = l.astype(BF16)
        l_lo = (l - l_hi.astype(F32)).astype(BF16)
        left[:, 0:depth] = l_hi
        left[:, depth : 2 * depth] = l_hi
        left[:, 2 * depth : 3 * depth] = l_lo
        a = amp_rows[...]
        a_hi = a.astype(BF16)
        a_lo = (a - a_hi.astype(F32)).astype(BF16)
        right[0:depth] = a_hi
        right[depth : 2 * depth] = a_lo
        right[2 * depth : 3 * depth] = a_hi
        mine = pl.ds(pl.multiple_of((HALF_LANES - HALF) * core, 64), HALF)
        out[...] += jnp.dot(left[mine, 0 : 3 * depth], right[0 : 3 * depth], preferred_element_type=F32)

    def tick(t, _):
        @pl.when(t + 2 < CHUNKS)
        def _():
            for side in sides:
                side.cross_own(t + 2)

        @pl.when(t + 1 < CHUNKS)
        def _():
            for side in sides:
                side.ring_own(t + 1)

        @pl.when(t < CHUNKS)
        def _():
            for side in sides:
                side.ring_partner(t)
            for side in sides:
                side.pass_own(t)

        @pl.when((t >= 1) & (t <= CHUNKS))
        def _():
            for side in sides:
                side.pass_partner(t - 1)

        @pl.when(t == 0)
        def _():
            for side in sides:
                side.pass_last()

        for step, at in enumerate(LAST_AT):

            @pl.when(t == at)
            def _(step=step):
                for side in sides:
                    side.cross_last(step)

        @pl.when((t >= 3) & (t < CHUNKS + 3))
        def _():
            for copy in share(t - 3):
                copy.wait_recv()
            multiply(lam_buf.at[t - 3], amp_buf.at[t - 3])

        @pl.when((t >= 2) & (t < CHUNKS + 2))
        def _():
            for side in sides:
                side.got(t - 2, 3, 4)
            for copy in share(t - 2):
                copy.start()

        @pl.when(t == CHUNKS)
        def _():
            for side in sides:
                for step in range(4):
                    side.got_last(3 + step)
            for copy in share_last():
                copy.start()

        @pl.when(t == CHUNKS + 1)
        def _():
            for copy in share_last():
                copy.wait_recv()
            multiply(lam_last, amp_last)

        @pl.when(t >= 3)
        def _():
            for side in sides:
                side.sent(t - 3)
            for copy in share(t - 3):
                copy.wait_send()

        return 0

    lax.fori_loop(0, CHUNKS + 3, tick, 0)
    for side in sides:
        side.sent_last()
    for copy in share_last():
        copy.wait_send()


def gather_multiply(lambdas, amplitudes):
    dma = pltpu.SemaphoreType.DMA
    return pl.pallas_call(
        kernel,
        out_shape=jax.ShapeDtypeStruct((HALF, WIDTH), F32),
        in_specs=[pl.BlockSpec(memory_space=pl.ANY)] * 2,
        out_specs=pl.BlockSpec(memory_space=pltpu.VMEM),
        scratch_shapes=[
            pltpu.VMEM((CHUNKS, 2 * SOURCES * ROWS, WIDTH), F32),
            pltpu.VMEM((CHUNKS, 2 * SOURCES * ROWS, WIDTH), F32),
            pltpu.VMEM((2 * SOURCES * LAST_ROWS, WIDTH), F32),
            pltpu.VMEM((2 * SOURCES * LAST_ROWS, WIDTH), F32),
            pltpu.VMEM((HALF_LANES, 3 * 2 * SOURCES * LAST_ROWS), BF16),
            pltpu.VMEM((3 * 2 * SOURCES * LAST_ROWS, WIDTH), BF16),
            dma((2,)),
            dma((CHUNKS,)),
            dma((CHUNKS,)),
            dma((CHUNKS, 4)),
            dma((CHUNKS, 4)),
            dma,
            dma,
            dma((7,)),
            dma((7,)),
            dma((CHUNKS, 2)),
            dma((CHUNKS, 2)),
            dma((2,)),
            dma((2,)),
        ],
        compiler_params=pltpu.CompilerParams(collective_id=0, has_side_effects=True, vmem_limit_bytes=58 << 20),
        cost_estimate=pl.CostEstimate(flops=6 * 3200 * HALF * WIDTH, bytes_accessed=8 << 20, transcendentals=0),
    )(lambdas, amplitudes)


def lookup(index, virt_irrep):
    table = jnp.arange(virt_irrep.shape[0], dtype=jnp.int32)
    match = index[:, None] == table[None, :]
    return jnp.sum(jnp.where(match, virt_irrep[None, :], 0), axis=1)


def pair_signs(first, second, virt_irrep):
    return jnp.where(lookup(first, virt_irrep) > lookup(second, virt_irrep), -1.0, 1.0).astype(F32)


def on_device(lambdas, amplitudes, virt_irrep, ab_first, ab_second, cd_first, cd_second):
    sign_ab = pair_signs(ab_first, ab_second, virt_irrep)
    sign_cd = pair_signs(cd_first, cd_second, virt_irrep)
    gamma_sum = gather_multiply(lambdas, amplitudes)
    return gamma_sum * sign_ab[:, None] * sign_cd[None, :]


def solution(mesh):
    return jax.shard_map(
        on_device,
        mesh=mesh,
        in_specs=(
            P(("col", "depth"), "row"),
            P(("row", "depth"), "col"),
            P(),
            P(("row", "depth")),
            P(("row", "depth")),
            P("col"),
            P("col"),
        ),
        out_specs=P(("row", "depth"), "col"),
        check_vma=False,
    )
```

```python
import functools

import jax
import jax.numpy as jnp
from jax import lax
from jax.experimental import pallas as pl
from jax.experimental.pallas import tpu as pltpu
from jax.sharding import PartitionSpec as P

MESH = pl.DeviceIdType.MESH
F32, BF16, I32 = jnp.float32, jnp.bfloat16, jnp.int32

MAIN, MAIN_ROWS = 11, 16
SMALL, SMALL_ROWS = 1, 8
CHUNKS = MAIN + SMALL
LAST_ROWS = 16
LAST_AT = (0, 3, 6, 8)
LAST_SHARE, LAST_MULTIPLY = 10, 11
SOURCES = 8
WIDTH = 1408
HALF = 704
HALF_LANES = 768
HALF_AT = 640
ORBITALS = 1200
TABLE = 1280


class Chunk:
    def __init__(self, side, buf, rows, start, send, recv):
        self.side, self.buf, self.rows, self.start, self.send, self.recv = side, buf, rows, start, send, recv

    def at(self, block):
        first = (self.side.core * SOURCES + block) * self.rows
        return self.buf.at[pl.ds(pl.multiple_of(first, 8), self.rows)]

    def own(self):
        return self.side.own.at[pl.ds(pl.multiple_of(self.start, 8), self.rows)]

    def lay(self, sem):
        pltpu.make_async_copy(self.own(), self.at(self.side.me), sem).start()

    def put(self, block, target, kind, own=False):
        here = self.at(block)
        pltpu.make_async_remote_copy(
            src_ref=self.own() if own else here,
            dst_ref=here,
            send_sem=self.send,
            recv_sem=self.recv(kind),
            device_id=self.side.device(target),
            device_id_type=MESH,
        ).start()

    def wait(self, sem, blocks):
        part = self.buf.at[pl.ds(0, blocks * self.rows)]
        pltpu.make_async_copy(part, part, sem).wait()

    def got(self, kind, blocks=1):
        self.wait(self.recv(kind), blocks)

    def sent(self):
        self.wait(self.send, 7)

    def cross_own(self):
        self.put(self.side.me, self.side.plane(self.side.me), 0, own=True)

    def ring_own(self):
        side = self.side
        self.put(side.me, side.ring(side.me, side.way), 1, own=True)
        self.put(side.me, side.ring(side.me, -side.way), 3, own=True)

    def ring_partner(self):
        side = self.side
        self.got(0)
        block = side.plane(side.me)
        self.put(block, side.ring(side.me, side.way), 2)
        self.put(block, side.ring(side.me, -side.way), 3)

    def pass_own(self):
        side = self.side
        self.got(1)
        self.put(side.ring(side.me, -side.way), side.ring(side.me, side.way), 3)

    def pass_partner(self):
        side = self.side
        self.got(2)
        self.put(side.plane(side.ring(side.me, -side.way)), side.ring(side.me, side.way), 4)

    def ring_last(self):
        side = self.side
        self.put(side.me, side.ring(side.me, side.way), 0, own=True)
        self.put(side.me, side.ring(side.me, -side.way), 1, own=True)

    def pass_last(self):
        side = self.side
        self.got(0)
        self.put(side.ring(side.me, -side.way), side.ring(side.me, side.way), 2)

    def cross_last(self, step):
        side = self.side
        if step >= 2:
            self.got(step - 1)
        offset = (0, -side.way, side.way, 2)[step]
        self.put(side.ring(side.me, offset), side.plane(side.me), 3 + step)


class Side:
    def __init__(self, own, core, me, ring, plane, device):
        self.own, self.core, self.me = own, core, me
        self.ring, self.plane, self.device = ring, plane, device
        self.way = 1 - 2 * core


def set_signs(virt, first, second, row_out, table_col):
    tile = lax.broadcasted_iota(I32, (TABLE, 128), 0)
    full = first.shape[0]
    for at in range(0, full, 128):
        width = min(128, full - at)
        lanes = pl.ds(at, width)
        held = table_col[:, 0:width]
        rows = tile[:, 0:width]
        of_first = jnp.where(rows == first[lanes].reshape(1, width), held, 0.0)
        of_second = jnp.where(rows == second[lanes].reshape(1, width), held, 0.0)
        gap = jnp.sum(of_first - of_second, axis=0, keepdims=True)
        row_out[0:1, lanes] = jnp.where(gap > 0.0, -1.0, 1.0)


def kernel(
    lam, amp, virt, ab_first, ab_second, cd_first, cd_second, out,
    lam_main, amp_main, lam_small, amp_small, lam_last, amp_last, left, right,
    table_row, table_col, ab_row, ab_col, cd_row,
    local_sem, main_send, main_recv, small_send, small_recv, last_send, last_recv,
    core_send, core_recv, small_core_send, small_core_recv, last_core_send, last_core_recv,
):
    row, col, core = lax.axis_index("row"), lax.axis_index("col"), lax.axis_index("depth")
    lam_side = Side(
        lam, core, col,
        lambda k, s: (k + 2 * s + 8) % 8,
        lambda k: k + 1 - 2 * (k % 2),
        lambda k: (row, k, core),
    )
    amp_side = Side(
        amp, core, row,
        lambda k, s: k // 4 * 4 + (k + s + 4) % 4,
        lambda k: (k + 4) % 8,
        lambda k: (k, col, core),
    )
    sides = (lam_side, amp_side)
    other = (row, col, 1 - core)

    barrier = pltpu.get_barrier_semaphore()
    partners = [other]
    for side in sides:
        partners += [side.device(k) for k in (side.plane(side.me), side.ring(side.me, 1), side.ring(side.me, -1))]
    for partner in partners:
        pl.semaphore_signal(barrier, inc=1, device_id=partner, device_id_type=MESH)

    table_row[...] = jnp.zeros_like(table_row)
    table_row[0:1, 0:ORBITALS] = virt[...].astype(F32).reshape(1, ORBITALS)
    table_col[...] = jnp.broadcast_to(table_row[0:1, :], (128, TABLE)).T
    ab_row[...] = jnp.ones_like(ab_row)
    set_signs(virt, ab_first, ab_second, ab_row, table_col)
    set_signs(virt, cd_first, cd_second, cd_row, table_col)
    shifted = pltpu.roll(ab_row[...], (HALF_LANES - HALF) * core, 1)
    ab_col[...] = jnp.broadcast_to(shifted[0:1, :], (128, HALF_LANES)).T
    out[...] = jnp.zeros_like(out)
    pl.semaphore_wait(barrier, len(partners))

    def main(j):
        return [
            Chunk(side, buf.at[j], MAIN_ROWS, j * MAIN_ROWS, main_send.at[i, j], lambda k, i=i: main_recv.at[i, j, k])
            for i, (side, buf) in enumerate(zip(sides, (lam_main, amp_main)))
        ]

    def small(j):
        start = MAIN * MAIN_ROWS + j * SMALL_ROWS
        return [
            Chunk(side, buf.at[j], SMALL_ROWS, start, small_send.at[i, j], lambda k, i=i: small_recv.at[i, j, k])
            for i, (side, buf) in enumerate(zip(sides, (lam_small, amp_small)))
        ]

    start = MAIN * MAIN_ROWS + SMALL * SMALL_ROWS
    last = [
        Chunk(side, buf, LAST_ROWS, start, last_send.at[i], lambda k, i=i: last_recv.at[i, k])
        for i, (side, buf) in enumerate(zip(sides, (lam_last, amp_last)))
    ]

    def on_chunk(j, do):
        @pl.when((j >= 0) & (j < MAIN))
        def _():
            for chunk in main(j):
                do(chunk)

        @pl.when((j >= MAIN) & (j < CHUNKS))
        def _():
            for chunk in small(j - MAIN):
                do(chunk)

    for chunk in main(0):
        chunk.cross_own()
    for chunk in main(0):
        chunk.ring_own()
    for chunk in last:
        chunk.ring_last()
    for chunk in main(1):
        chunk.cross_own()

    def lay(j, _):
        for i, chunk in enumerate(main(j)):
            chunk.lay(local_sem.at[i])
        return 0

    lax.fori_loop(0, MAIN, lay, 0)
    for j in range(SMALL):
        for i, chunk in enumerate(small(j)):
            chunk.lay(local_sem.at[i])
    for i, chunk in enumerate(last):
        chunk.lay(local_sem.at[i])
    for i, side in enumerate(sides):
        pltpu.make_async_copy(side.own, side.own, local_sem.at[i]).wait()

    def lanes(of):
        return pl.ds(pl.multiple_of(HALF_AT * of, 128), HALF_LANES)

    def to_core(parts, send, recv):
        return [
            pltpu.make_async_remote_copy(
                src_ref=part, dst_ref=part, send_sem=send.at[i], recv_sem=recv.at[i], device_id=other, device_id_type=MESH
            )
            for i, part in enumerate(parts)
        ]

    def share(chunks, send, recv):
        lam_chunk, amp_chunk = chunks
        rows = SOURCES * lam_chunk.rows
        mine = pl.ds(pl.multiple_of(core * rows, 64), rows)
        return to_core((lam_chunk.buf.at[mine, lanes(1 - core)], amp_chunk.buf.at[mine]), send, recv)

    def share_main(j):
        return share(main(j), core_send.at[j], core_recv.at[j])

    def share_last():
        return share(last, last_core_send, last_core_recv)

    def share_block(chunks, block_of, send, recv):
        lam_chunk, amp_chunk = chunks
        parts = (lam_chunk.at(block_of(lam_side)).at[:, lanes(1 - core)], amp_chunk.at(block_of(amp_side)))
        return to_core(parts, send, recv)

    def far(side):
        return side.plane(side.ring(side.me, 2))

    def share_early(j):
        copies = []
        for s in (0, 1, -1, 2):
            copies += share_block(small(j), lambda side: side.ring(side.me, s), small_core_send.at[j], small_core_recv.at[j, 0])
            if s != 2:
                copies += share_block(
                    small(j), lambda side: side.plane(side.ring(side.me, s)), small_core_send.at[j], small_core_recv.at[j, 0]
                )
        return copies

    def share_far(j):
        return share_block(small(j), far, small_core_send.at[j], small_core_recv.at[j, 1])

    def small_wait(j, sem, blocks):
        lam_chunk, amp_chunk = small(j)
        rows = pl.ds(0, blocks * SMALL_ROWS)
        for i, part in enumerate((lam_chunk.buf.at[rows, lanes(0)], amp_chunk.buf.at[rows])):
            pltpu.make_async_copy(part, part, sem.at[i]).wait()

    def multiply(lam_rows, amp_rows):
        depth = lam_rows.shape[0]
        l = lam_rows[:, lanes(core)].T * jnp.concatenate([ab_col[...]] * (depth // 128), axis=1)
        l_hi = l.astype(BF16)
        l_lo = (l - l_hi.astype(F32)).astype(BF16)
        left[:, 0:depth] = l_hi
        left[:, depth : 2 * depth] = l_hi
        left[:, 2 * depth : 3 * depth] = l_lo
        a = amp_rows[...] * cd_row[0:1, :]
        a_hi = a.astype(BF16)
        a_lo = (a - a_hi.astype(F32)).astype(BF16)
        right[0:depth] = a_hi
        right[depth : 2 * depth] = a_lo
        right[2 * depth : 3 * depth] = a_hi
        mine = pl.ds(pl.multiple_of((HALF_LANES - HALF) * core, 64), HALF)
        out[...] += jnp.dot(left[mine, 0 : 3 * depth], right[0 : 3 * depth], preferred_element_type=F32)

    def tick(t, _):
        on_chunk(t + 2, lambda chunk: chunk.cross_own())
        on_chunk(t + 1, lambda chunk: chunk.ring_own())
        on_chunk(t, lambda chunk: chunk.ring_partner())
        on_chunk(t, lambda chunk: chunk.pass_own())
        on_chunk(t - 1, lambda chunk: chunk.pass_partner())

        @pl.when(t == 0)
        def _():
            for chunk in last:
                chunk.pass_last()

        for step, at in enumerate(LAST_AT):

            @pl.when(t == at)
            def _(step=step):
                for chunk in last:
                    chunk.cross_last(step)

        @pl.when((t >= 3) & (t < MAIN + 3))
        def _():
            for copy in share_main(t - 3):
                copy.wait_recv()
            multiply(lam_main.at[t - 3], amp_main.at[t - 3])

        @pl.when((t >= 2) & (t < MAIN + 2))
        def _():
            for chunk in main(t - 2):
                chunk.got(3, 3)
                chunk.got(4)
            for copy in share_main(t - 2):
                copy.start()

        @pl.when(t == LAST_SHARE)
        def _():
            for chunk in last:
                for step in range(4):
                    chunk.got(3 + step)
            for copy in share_last():
                copy.start()

        @pl.when(t == LAST_MULTIPLY)
        def _():
            for copy in share_last():
                copy.wait_recv()
            multiply(lam_last, amp_last)

        @pl.when((t >= MAIN + 1) & (t < CHUNKS + 1))
        def _():
            j = t - 1 - MAIN
            for chunk in small(j):
                chunk.got(3, 3)
            for copy in share_early(j):
                copy.start()

        @pl.when((t >= MAIN + 2) & (t < CHUNKS + 2))
        def _():
            j = t - 2 - MAIN
            for chunk in small(j):
                chunk.got(4)
            for copy in share_far(j):
                copy.start()
            small_wait(j, small_core_recv.at[j, 0], 7)
            small_wait(j, small_core_recv.at[j, 1], 1)
            multiply(lam_small.at[j], amp_small.at[j])

        @pl.when((t >= 3) & (t < MAIN + 3))
        def _():
            for chunk in main(t - 3):
                chunk.sent()
            for copy in share_main(t - 3):
                copy.wait_send()

        return 0

    lax.fori_loop(0, max(CHUNKS + 2, MAIN + 3), tick, 0)
    for j in range(SMALL):
        for chunk in small(j):
            chunk.sent()
        small_wait(j, small_core_send.at[j], 8)
    for chunk in last:
        chunk.sent()
    for copy in share_last():
        copy.wait_send()


def gather_multiply(lambdas, amplitudes, virt_irrep, ab_first, ab_second, cd_first, cd_second):
    dma = pltpu.SemaphoreType.DMA
    most = 3 * 2 * SOURCES * max(MAIN_ROWS, SMALL_ROWS, LAST_ROWS)
    rows = [virt_irrep, ab_first, ab_second, cd_first, cd_second]
    buffers = [
        pltpu.VMEM(shape, F32)
        for shape in (
            (MAIN, 2 * SOURCES * MAIN_ROWS, WIDTH),
            (SMALL, 2 * SOURCES * SMALL_ROWS, WIDTH),
            (2 * SOURCES * LAST_ROWS, WIDTH),
        )
        for _ in range(2)
    ]
    return pl.pallas_call(
        kernel,
        out_shape=pltpu.VMEM((HALF, WIDTH), F32),
        in_specs=[pl.BlockSpec(memory_space=pl.ANY)] * 2 + [pl.BlockSpec(memory_space=pltpu.VMEM)] * 5,
        out_specs=pl.BlockSpec(memory_space=pltpu.VMEM),
        scratch_shapes=buffers
        + [
            pltpu.VMEM((HALF_LANES, most), BF16),
            pltpu.VMEM((most, WIDTH), BF16),
            pltpu.VMEM((8, TABLE), F32),
            pltpu.VMEM((TABLE, 128), F32),
            pltpu.VMEM((8, HALF_LANES), F32),
            pltpu.VMEM((HALF_LANES, 128), F32),
            pltpu.VMEM((8, WIDTH), F32),
            dma((2,)),
            dma((2, MAIN)),
            dma((2, MAIN, 5)),
            dma((2, SMALL)),
            dma((2, SMALL, 5)),
            dma((2,)),
            dma((2, 7)),
            dma((MAIN, 2)),
            dma((MAIN, 2)),
            dma((SMALL, 2)),
            dma((SMALL, 2, 2)),
            dma((2,)),
            dma((2,)),
        ],
        compiler_params=pltpu.CompilerParams(collective_id=0, has_side_effects=True, vmem_limit_bytes=54 << 20),
        cost_estimate=pl.CostEstimate(flops=6 * 3200 * HALF * WIDTH, bytes_accessed=8 << 20, transcendentals=0),
    )(lambdas, amplitudes, *rows)


def solution(mesh):
    return jax.shard_map(
        gather_multiply,
        mesh=mesh,
        in_specs=(
            P(("col", "depth"), "row"),
            P(("row", "depth"), "col"),
            P(),
            P(("row", "depth")),
            P(("row", "depth")),
            P("col"),
            P("col"),
        ),
        out_specs=P(("row", "depth"), "col"),
        check_vma=False,
    )
```

```python
import functools

import jax
import jax.numpy as jnp
from jax import lax
from jax.experimental import pallas as pl
from jax.experimental.pallas import tpu as pltpu
from jax.sharding import PartitionSpec as P

MESH = pl.DeviceIdType.MESH
F32, BF16, I32 = jnp.float32, jnp.bfloat16, jnp.int32

MAIN, MAIN_ROWS = 11, 16
SMALL, SMALL_ROWS = 1, 8
CHUNKS = MAIN + SMALL
LAST_ROWS = 16
LAST_AT = (0, 2, 4, 7)
LAST_SHARE, LAST_MULTIPLY = 9, 10
SHARE_LAG = 3
SOURCES = 8
WIDTH = 1408
HALF = 704
HALF_LANES = 768
HALF_AT = 640
ORBITALS = 1200
TABLE = 1280


class Chunk:
    def __init__(self, side, buf, rows, start, send, recv):
        self.side, self.buf, self.rows, self.start, self.send, self.recv = side, buf, rows, start, send, recv

    def at(self, block):
        first = (self.side.core * SOURCES + block) * self.rows
        return self.buf.at[pl.ds(pl.multiple_of(first, 8), self.rows)]

    def own(self):
        return self.side.own.at[pl.ds(pl.multiple_of(self.start, 8), self.rows)]

    def lay(self, sem):
        pltpu.make_async_copy(self.own(), self.at(self.side.me), sem).start()

    def put(self, block, target, kind, own=False):
        here = self.at(block)
        pltpu.make_async_remote_copy(
            src_ref=self.own() if own else here,
            dst_ref=here,
            send_sem=self.send,
            recv_sem=self.recv(kind),
            device_id=self.side.device(target),
            device_id_type=MESH,
        ).start()

    def wait(self, sem, blocks):
        part = self.buf.at[pl.ds(0, blocks * self.rows)]
        pltpu.make_async_copy(part, part, sem).wait()

    def got(self, kind, blocks=1):
        self.wait(self.recv(kind), blocks)

    def sent(self):
        self.wait(self.send, 7)

    def cross_own(self):
        self.put(self.side.me, self.side.pair, 0, own=True)

    def ring_own(self):
        side = self.side
        self.put(side.me, side.ahead, 1, own=True)
        self.put(side.me, side.behind, 3, own=True)

    def ring_partner(self):
        side = self.side
        self.got(0)
        block = side.pair
        self.put(block, side.ahead, 2)
        self.put(block, side.behind, 3)

    def pass_own(self):
        side = self.side
        self.got(1)
        self.put(side.behind, side.ahead, 3)

    def pass_partner(self):
        side = self.side
        self.got(2)
        self.put(side.pair_behind, side.ahead, 4)

    def ring_last(self):
        side = self.side
        self.put(side.me, side.ahead, 0, own=True)
        self.put(side.me, side.behind, 1, own=True)

    def pass_last(self):
        side = self.side
        self.got(0)
        self.put(side.behind, side.ahead, 2)

    def cross_last(self, step):
        side = self.side
        if step >= 2:
            self.got(step - 1)
        block = (side.me, side.behind, side.ahead, side.opposite)[step]
        self.put(block, side.pair, 3 + step)


class Side:
    def __init__(self, own, core, me, ring, plane, device):
        self.own, self.core, self.me = own, core, me
        self.device = device
        way = 1 - 2 * core
        self.ahead, self.behind, self.opposite = ring(me, way), ring(me, -way), ring(me, 2)
        self.pair, self.pair_ahead, self.pair_behind = plane(me), plane(self.ahead), plane(self.behind)
        self.far = plane(self.opposite)


def set_signs(virt, first, second, row_out, table_col):
    tile = lax.broadcasted_iota(I32, (TABLE, 128), 0)
    full = first.shape[0]
    for at in range(0, full, 128):
        width = min(128, full - at)
        lanes = pl.ds(at, width)
        held = table_col[:, 0:width]
        rows = tile[:, 0:width]
        of_first = jnp.where(rows == first[lanes].reshape(1, width), held, 0.0)
        of_second = jnp.where(rows == second[lanes].reshape(1, width), held, 0.0)
        gap = jnp.sum(of_first - of_second, axis=0, keepdims=True)
        row_out[0:1, lanes] = jnp.where(gap > 0.0, -1.0, 1.0)


def kernel(
    lam, amp, virt_in, ab_first_in, ab_second_in, cd_first_in, cd_second_in, out,
    virt, ab_first, ab_second, cd_first, cd_second,
    lam_main, amp_main, lam_small, amp_small, lam_last, amp_last, left, right,
    table_row, table_col, ab_row, ab_col, cd_row,
    local_sem, main_send, main_recv, small_send, small_recv, last_send, last_recv,
    core_send, core_recv, small_core_send, small_core_recv, last_core_send, last_core_recv,
):
    row, col, core = lax.axis_index("row"), lax.axis_index("col"), lax.axis_index("depth")
    lam_side = Side(
        lam, core, col,
        lambda k, s: (k + 2 * s + 8) % 8,
        lambda k: k + 1 - 2 * (k % 2),
        lambda k: (row, k, core),
    )
    amp_side = Side(
        amp, core, row,
        lambda k, s: k // 4 * 4 + (k + s + 4) % 4,
        lambda k: (k + 4) % 8,
        lambda k: (k, col, core),
    )
    sides = (lam_side, amp_side)
    other = (row, col, 1 - core)

    barrier = pltpu.get_barrier_semaphore()
    partners = [other]
    for side in sides:
        partners += [side.device(k) for k in (side.pair, side.ahead, side.behind)]
    for partner in partners:
        pl.semaphore_signal(barrier, inc=1, device_id=partner, device_id_type=MESH)

    staged = [
        pltpu.make_async_copy(src, dst, local_sem.at[2 + i])
        for i, (src, dst) in enumerate(
            (
                (virt_in, virt),
                (ab_first_in, ab_first),
                (ab_second_in, ab_second),
                (cd_first_in, cd_first),
                (cd_second_in, cd_second),
            )
        )
    ]
    for copy in staged:
        copy.start()
    pl.semaphore_wait(barrier, len(partners))

    def main(j):
        return [
            Chunk(side, buf.at[j], MAIN_ROWS, j * MAIN_ROWS, main_send.at[i, j], lambda k, i=i: main_recv.at[i, j, k])
            for i, (side, buf) in enumerate(zip(sides, (lam_main, amp_main)))
        ]

    def small(j):
        start = MAIN * MAIN_ROWS + j * SMALL_ROWS
        return [
            Chunk(side, buf.at[j], SMALL_ROWS, start, small_send.at[i, j], lambda k, i=i: small_recv.at[i, j, k])
            for i, (side, buf) in enumerate(zip(sides, (lam_small, amp_small)))
        ]

    start = MAIN * MAIN_ROWS + SMALL * SMALL_ROWS
    last = [
        Chunk(side, buf, LAST_ROWS, start, last_send.at[i], lambda k, i=i: last_recv.at[i, k])
        for i, (side, buf) in enumerate(zip(sides, (lam_last, amp_last)))
    ]

    def on_chunk(j, do):
        @pl.when((j >= 0) & (j < MAIN))
        def _():
            for chunk in main(j):
                do(chunk)

        @pl.when((j >= MAIN) & (j < CHUNKS))
        def _():
            for chunk in small(j - MAIN):
                do(chunk)

    for chunk in main(0):
        chunk.cross_own()
    for chunk in main(0):
        chunk.ring_own()
    for chunk in last:
        chunk.ring_last()
    for chunk in main(1):
        chunk.cross_own()

    def lay(j, _):
        for i, chunk in enumerate(main(j)):
            chunk.lay(local_sem.at[i])
        return 0

    lax.fori_loop(0, MAIN, lay, 0)
    for j in range(SMALL):
        for i, chunk in enumerate(small(j)):
            chunk.lay(local_sem.at[i])
    for i, chunk in enumerate(last):
        chunk.lay(local_sem.at[i])
    for copy in staged:
        copy.wait()
    table_row[...] = jnp.zeros_like(table_row)
    table_row[0:1, 0:ORBITALS] = virt[...].astype(F32).reshape(1, ORBITALS)
    table_col[...] = jnp.broadcast_to(table_row[0:1, :], (128, TABLE)).T
    ab_row[...] = jnp.ones_like(ab_row)
    set_signs(virt, ab_first, ab_second, ab_row, table_col)
    set_signs(virt, cd_first, cd_second, cd_row, table_col)
    shifted = pltpu.roll(ab_row[...], (HALF_LANES - HALF) * core, 1)
    ab_col[...] = jnp.broadcast_to(shifted[0:1, :], (128, HALF_LANES)).T
    out[...] = jnp.zeros_like(out)
    for i, side in enumerate(sides):
        pltpu.make_async_copy(side.own, side.own, local_sem.at[i]).wait()

    def lanes(of):
        return pl.ds(pl.multiple_of(HALF_AT * of, 128), HALF_LANES)

    def to_core(parts, send, recv):
        return [
            pltpu.make_async_remote_copy(
                src_ref=part, dst_ref=part, send_sem=send.at[i], recv_sem=recv.at[i], device_id=other, device_id_type=MESH
            )
            for i, part in enumerate(parts)
        ]

    def share(chunks, send, recv):
        lam_chunk, amp_chunk = chunks
        rows = SOURCES * lam_chunk.rows
        mine = pl.ds(pl.multiple_of(core * rows, 64), rows)
        return to_core((lam_chunk.buf.at[mine, lanes(1 - core)], amp_chunk.buf.at[mine]), send, recv)

    def share_main(j):
        return share(main(j), core_send.at[j], core_recv.at[j])

    def share_last():
        return share(last, last_core_send, last_core_recv)

    def share_block(chunks, block_of, send, recv):
        lam_chunk, amp_chunk = chunks
        parts = (lam_chunk.at(block_of(lam_side)).at[:, lanes(1 - core)], amp_chunk.at(block_of(amp_side)))
        return to_core(parts, send, recv)

    def far(side):
        return side.far

    def share_early(j):
        copies = []
        for name in ("me", "ahead", "behind", "opposite", "pair", "pair_ahead", "pair_behind"):
            copies += share_block(small(j), lambda side, name=name: getattr(side, name), small_core_send.at[j], small_core_recv.at[j, 0])
        return copies

    def share_far(j):
        return share_block(small(j), far, small_core_send.at[j], small_core_recv.at[j, 1])

    def small_wait(j, sem, blocks):
        lam_chunk, amp_chunk = small(j)
        rows = pl.ds(0, blocks * SMALL_ROWS)
        for i, part in enumerate((lam_chunk.buf.at[rows, lanes(0)], amp_chunk.buf.at[rows])):
            pltpu.make_async_copy(part, part, sem.at[i]).wait()

    def multiply(lam_rows, amp_rows):
        depth = lam_rows.shape[0]
        l = lam_rows[:, lanes(core)].T * jnp.concatenate([ab_col[...]] * (depth // 128), axis=1)
        l_hi = l.astype(BF16)
        l_lo = (l - l_hi.astype(F32)).astype(BF16)
        left[:, 0:depth] = l_hi
        left[:, depth : 2 * depth] = l_hi
        left[:, 2 * depth : 3 * depth] = l_lo
        a = amp_rows[...] * cd_row[0:1, :]
        a_hi = a.astype(BF16)
        a_lo = (a - a_hi.astype(F32)).astype(BF16)
        right[0:depth] = a_hi
        right[depth : 2 * depth] = a_lo
        right[2 * depth : 3 * depth] = a_hi
        mine = pl.ds(pl.multiple_of((HALF_LANES - HALF) * core, 64), HALF)
        out[...] += jnp.dot(left[mine, 0 : 3 * depth], right[0 : 3 * depth], preferred_element_type=F32)

    def tick(t, _):
        on_chunk(t + 2, lambda chunk: chunk.cross_own())
        on_chunk(t + 1, lambda chunk: chunk.ring_own())
        on_chunk(t, lambda chunk: chunk.ring_partner())
        on_chunk(t, lambda chunk: chunk.pass_own())

        @pl.when(t < CHUNKS)
        def _():
            on_chunk(t - 2, lambda chunk: chunk.pass_partner())

        @pl.when(t == CHUNKS - 1)
        def _():
            for chunk in main(MAIN - 1):
                chunk.pass_partner()

        @pl.when(t == CHUNKS)
        def _():
            for chunk in small(SMALL - 1):
                chunk.pass_partner()

        @pl.when(t == 0)
        def _():
            for chunk in last:
                chunk.pass_last()

        for step, at in enumerate(LAST_AT):

            @pl.when(t == at)
            def _(step=step):
                for chunk in last:
                    chunk.cross_last(step)

        @pl.when(t == LAST_SHARE)
        def _():
            for chunk in last:
                for step in range(4):
                    chunk.got(3 + step)
            for copy in share_last():
                copy.start()

        @pl.when(t == LAST_MULTIPLY)
        def _():
            for copy in share_last():
                copy.wait_recv()
            multiply(lam_last, amp_last)

        @pl.when((t >= SHARE_LAG) & (t < MAIN + SHARE_LAG))
        def _():
            j = t - SHARE_LAG
            for chunk in main(j):
                chunk.got(3, 3)
                chunk.got(4)
            for copy in share_main(j):
                copy.start()

        @pl.when((t >= MAIN + SHARE_LAG) & (t < CHUNKS + SHARE_LAG))
        def _():
            j = t - SHARE_LAG - MAIN
            for chunk in small(j):
                chunk.got(3, 3)
            for copy in share_early(j):
                copy.start()
            for chunk in small(j):
                chunk.got(4)
            for copy in share_far(j):
                copy.start()

        @pl.when((t >= SHARE_LAG + 1) & (t < MAIN + SHARE_LAG + 1))
        def _():
            j = t - SHARE_LAG - 1
            for copy in share_main(j):
                copy.wait_recv()
            multiply(lam_main.at[j], amp_main.at[j])
            for chunk in main(j):
                chunk.sent()
            for copy in share_main(j):
                copy.wait_send()

        @pl.when((t >= MAIN + SHARE_LAG + 1) & (t < CHUNKS + SHARE_LAG + 1))
        def _():
            j = t - SHARE_LAG - 1 - MAIN
            small_wait(j, small_core_recv.at[j, 0], 7)
            small_wait(j, small_core_recv.at[j, 1], 1)
            multiply(lam_small.at[j], amp_small.at[j])

        return 0

    lax.fori_loop(0, CHUNKS + SHARE_LAG + 1, tick, 0)
    for j in range(SMALL):
        for chunk in small(j):
            chunk.sent()
        small_wait(j, small_core_send.at[j], 8)
    for chunk in last:
        chunk.sent()
    for copy in share_last():
        copy.wait_send()


def gather_multiply(lambdas, amplitudes, virt_irrep, ab_first, ab_second, cd_first, cd_second):
    dma = pltpu.SemaphoreType.DMA
    most = 3 * 2 * SOURCES * max(MAIN_ROWS, SMALL_ROWS, LAST_ROWS)
    rows = [virt_irrep, ab_first, ab_second, cd_first, cd_second]
    buffers = [
        pltpu.VMEM(shape, F32)
        for shape in (
            (MAIN, 2 * SOURCES * MAIN_ROWS, WIDTH),
            (SMALL, 2 * SOURCES * SMALL_ROWS, WIDTH),
            (2 * SOURCES * LAST_ROWS, WIDTH),
        )
        for _ in range(2)
    ]
    return pl.pallas_call(
        kernel,
        out_shape=pltpu.VMEM((HALF, WIDTH), F32),
        in_specs=[pl.BlockSpec(memory_space=pl.ANY)] * 7,
        out_specs=pl.BlockSpec(memory_space=pltpu.VMEM),
        scratch_shapes=[pltpu.VMEM(x.shape, I32) for x in rows]
        + buffers
        + [
            pltpu.VMEM((HALF_LANES, most), BF16),
            pltpu.VMEM((most, WIDTH), BF16),
            pltpu.VMEM((8, TABLE), F32),
            pltpu.VMEM((TABLE, 128), F32),
            pltpu.VMEM((8, HALF_LANES), F32),
            pltpu.VMEM((HALF_LANES, 128), F32),
            pltpu.VMEM((8, WIDTH), F32),
            dma((7,)),
            dma((2, MAIN)),
            dma((2, MAIN, 5)),
            dma((2, SMALL)),
            dma((2, SMALL, 5)),
            dma((2,)),
            dma((2, 7)),
            dma((MAIN, 2)),
            dma((MAIN, 2)),
            dma((SMALL, 2)),
            dma((SMALL, 2, 2)),
            dma((2,)),
            dma((2,)),
        ],
        compiler_params=pltpu.CompilerParams(collective_id=0, has_side_effects=True, vmem_limit_bytes=54 << 20),
        cost_estimate=pl.CostEstimate(flops=6 * 3200 * HALF * WIDTH, bytes_accessed=8 << 20, transcendentals=0),
    )(lambdas, amplitudes, *rows)


def solution(mesh):
    return jax.shard_map(
        gather_multiply,
        mesh=mesh,
        in_specs=(
            P(("col", "depth"), "row"),
            P(("row", "depth"), "col"),
            P(),
            P(("row", "depth")),
            P(("row", "depth")),
            P("col"),
            P("col"),
        ),
        out_specs=P(("row", "depth"), "col"),
        check_vma=False,
    )
```

```python
import functools

import jax
import jax.numpy as jnp
from jax import lax
from jax.experimental import pallas as pl
from jax.experimental.pallas import tpu as pltpu
from jax.sharding import PartitionSpec as P

MESH = pl.DeviceIdType.MESH
F32, BF16, I32 = jnp.float32, jnp.bfloat16, jnp.int32

MAIN, MAIN_ROWS = 11, 16
SMALL, SMALL_ROWS = 1, 8
CHUNKS = MAIN + SMALL
LAST_ROWS = 16
LAST_AT = (0, 2, 4, 7)
LAST_SHARE, LAST_MULTIPLY = 9, 10
SOURCES = 8
WIDTH = 1408
HALF = 704
HALF_LANES = 768
HALF_AT = 640
ORBITALS = 1200
TABLE = 1280


class Chunk:
    def __init__(self, side, buf, rows, start, send, recv):
        self.side, self.buf, self.rows, self.start, self.send, self.recv = side, buf, rows, start, send, recv

    def at(self, block):
        first = (self.side.core * SOURCES + block) * self.rows
        return self.buf.at[pl.ds(pl.multiple_of(first, 8), self.rows)]

    def own(self):
        return self.side.own.at[pl.ds(pl.multiple_of(self.start, 8), self.rows)]

    def lay(self, sem):
        pltpu.make_async_copy(self.own(), self.at(self.side.me), sem).start()

    def put(self, block, target, kind, own=False):
        here = self.at(block)
        pltpu.make_async_remote_copy(
            src_ref=self.own() if own else here,
            dst_ref=here,
            send_sem=self.send,
            recv_sem=self.recv(kind),
            device_id=self.side.device(target),
            device_id_type=MESH,
        ).start()

    def wait(self, sem, blocks):
        part = self.buf.at[pl.ds(0, blocks * self.rows)]
        pltpu.make_async_copy(part, part, sem).wait()

    def got(self, kind, blocks=1):
        self.wait(self.recv(kind), blocks)

    def sent(self):
        self.wait(self.send, 7)

    def cross_own(self):
        self.put(self.side.me, self.side.pair, 0, own=True)

    def ring_own(self):
        side = self.side
        self.put(side.me, side.ahead, 1, own=True)
        self.put(side.me, side.behind, 3, own=True)

    def ring_partner(self):
        side = self.side
        self.got(0)
        block = side.pair
        self.put(block, side.ahead, 2)
        self.put(block, side.behind, 3)

    def pass_own(self):
        side = self.side
        self.got(1)
        self.put(side.behind, side.ahead, 3)

    def pass_partner(self):
        side = self.side
        self.got(2)
        self.put(side.pair_behind, side.ahead, 4)

    def ring_last(self):
        side = self.side
        self.put(side.me, side.ahead, 0, own=True)
        self.put(side.me, side.behind, 1, own=True)

    def pass_last(self):
        side = self.side
        self.got(0)
        self.put(side.behind, side.ahead, 2)

    def cross_last(self, step):
        side = self.side
        if step >= 2:
            self.got(step - 1)
        block = (side.me, side.behind, side.ahead, side.opposite)[step]
        self.put(block, side.pair, 3 + step)


class Side:
    def __init__(self, own, core, me, ring, plane, device):
        self.own, self.core, self.me = own, core, me
        self.device = device
        way = 1 - 2 * core
        self.ahead, self.behind, self.opposite = ring(me, way), ring(me, -way), ring(me, 2)
        self.pair, self.pair_ahead, self.pair_behind = plane(me), plane(self.ahead), plane(self.behind)
        self.far = plane(self.opposite)


def set_signs(virt, first, second, row_out, table_col):
    tile = lax.broadcasted_iota(I32, (TABLE, 128), 0)
    full = first.shape[0]
    for at in range(0, full, 128):
        width = min(128, full - at)
        lanes = pl.ds(at, width)
        held = table_col[:, 0:width]
        rows = tile[:, 0:width]
        of_first = jnp.where(rows == first[lanes].reshape(1, width), held, 0.0)
        of_second = jnp.where(rows == second[lanes].reshape(1, width), held, 0.0)
        gap = jnp.sum(of_first - of_second, axis=0, keepdims=True)
        row_out[0:1, lanes] = jnp.where(gap > 0.0, -1.0, 1.0)


def kernel(
    lam, amp, virt_in, ab_first_in, ab_second_in, cd_first_in, cd_second_in, out,
    virt, ab_first, ab_second, cd_first, cd_second,
    lam_main, amp_main, lam_small, amp_small, lam_last, amp_last, left, right,
    table_row, table_col, ab_row, ab_col, cd_row,
    local_sem, main_send, main_recv, small_send, small_recv, last_send, last_recv,
    core_send, core_recv, small_core_send, small_core_recv, last_core_send, last_core_recv,
):
    row, col, core = lax.axis_index("row"), lax.axis_index("col"), lax.axis_index("depth")
    lam_side = Side(
        lam, core, col,
        lambda k, s: (k + 2 * s + 8) % 8,
        lambda k: k + 1 - 2 * (k % 2),
        lambda k: (row, k, core),
    )
    amp_side = Side(
        amp, core, row,
        lambda k, s: k // 4 * 4 + (k + s + 4) % 4,
        lambda k: (k + 4) % 8,
        lambda k: (k, col, core),
    )
    sides = (lam_side, amp_side)
    other = (row, col, 1 - core)

    barrier = pltpu.get_barrier_semaphore()
    partners = [other]
    for side in sides:
        partners += [side.device(k) for k in (side.pair, side.ahead, side.behind)]
    for partner in partners:
        pl.semaphore_signal(barrier, inc=1, device_id=partner, device_id_type=MESH)

    staged = [
        pltpu.make_async_copy(src, dst, local_sem.at[2 + i])
        for i, (src, dst) in enumerate(
            (
                (virt_in, virt),
                (ab_first_in, ab_first),
                (ab_second_in, ab_second),
                (cd_first_in, cd_first),
                (cd_second_in, cd_second),
            )
        )
    ]
    for copy in staged:
        copy.start()
    pl.semaphore_wait(barrier, len(partners))

    def main(j):
        return [
            Chunk(side, buf.at[j], MAIN_ROWS, j * MAIN_ROWS, main_send.at[i, j], lambda k, i=i: main_recv.at[i, j, k])
            for i, (side, buf) in enumerate(zip(sides, (lam_main, amp_main)))
        ]

    def small(j):
        start = MAIN * MAIN_ROWS + j * SMALL_ROWS
        return [
            Chunk(side, buf.at[j], SMALL_ROWS, start, small_send.at[i, j], lambda k, i=i: small_recv.at[i, j, k])
            for i, (side, buf) in enumerate(zip(sides, (lam_small, amp_small)))
        ]

    start = MAIN * MAIN_ROWS + SMALL * SMALL_ROWS
    last = [
        Chunk(side, buf, LAST_ROWS, start, last_send.at[i], lambda k, i=i: last_recv.at[i, k])
        for i, (side, buf) in enumerate(zip(sides, (lam_last, amp_last)))
    ]

    def on_chunk(j, do):
        @pl.when((j >= 0) & (j < MAIN))
        def _():
            for chunk in main(j):
                do(chunk)

        @pl.when((j >= MAIN) & (j < CHUNKS))
        def _():
            for chunk in small(j - MAIN):
                do(chunk)

    for chunk in main(0):
        chunk.cross_own()
    for chunk in main(0):
        chunk.ring_own()
    for chunk in last:
        chunk.ring_last()
    for chunk in main(1):
        chunk.cross_own()

    def lay(j, _):
        for i, chunk in enumerate(main(j)):
            chunk.lay(local_sem.at[i])
        return 0

    lax.fori_loop(0, MAIN, lay, 0)
    for j in range(SMALL):
        for i, chunk in enumerate(small(j)):
            chunk.lay(local_sem.at[i])
    for i, chunk in enumerate(last):
        chunk.lay(local_sem.at[i])
    for copy in staged:
        copy.wait()
    table_row[...] = jnp.zeros_like(table_row)
    table_row[0:1, 0:ORBITALS] = virt[...].astype(F32).reshape(1, ORBITALS)
    table_col[...] = jnp.broadcast_to(table_row[0:1, :], (128, TABLE)).T
    ab_row[...] = jnp.ones_like(ab_row)
    set_signs(virt, ab_first, ab_second, ab_row, table_col)
    set_signs(virt, cd_first, cd_second, cd_row, table_col)
    shifted = pltpu.roll(ab_row[...], (HALF_LANES - HALF) * core, 1)
    ab_col[...] = jnp.broadcast_to(shifted[0:1, :], (128, HALF_LANES)).T
    out[...] = jnp.zeros_like(out)
    for i, side in enumerate(sides):
        pltpu.make_async_copy(side.own, side.own, local_sem.at[i]).wait()

    def lanes(of):
        return pl.ds(pl.multiple_of(HALF_AT * of, 128), HALF_LANES)

    def to_core(parts, send, recv):
        return [
            pltpu.make_async_remote_copy(
                src_ref=part, dst_ref=part, send_sem=send.at[i], recv_sem=recv.at[i], device_id=other, device_id_type=MESH
            )
            for i, part in enumerate(parts)
        ]

    def share(chunks, send, recv):
        lam_chunk, amp_chunk = chunks
        rows = SOURCES * lam_chunk.rows
        mine = pl.ds(pl.multiple_of(core * rows, 64), rows)
        return to_core((lam_chunk.buf.at[mine, lanes(1 - core)], amp_chunk.buf.at[mine]), send, recv)

    def share_main(j):
        return share(main(j), core_send.at[j], core_recv.at[j])

    def share_last():
        return share(last, last_core_send, last_core_recv)

    def share_block(chunks, block_of, send, recv):
        lam_chunk, amp_chunk = chunks
        parts = (lam_chunk.at(block_of(lam_side)).at[:, lanes(1 - core)], amp_chunk.at(block_of(amp_side)))
        return to_core(parts, send, recv)

    def far(side):
        return side.far

    def share_early(j):
        copies = []
        for name in ("me", "ahead", "behind", "opposite", "pair", "pair_ahead", "pair_behind"):
            copies += share_block(small(j), lambda side, name=name: getattr(side, name), small_core_send.at[j], small_core_recv.at[j, 0])
        return copies

    def share_far(j):
        return share_block(small(j), far, small_core_send.at[j], small_core_recv.at[j, 1])

    def small_wait(j, sem, blocks):
        lam_chunk, amp_chunk = small(j)
        rows = pl.ds(0, blocks * SMALL_ROWS)
        for i, part in enumerate((lam_chunk.buf.at[rows, lanes(0)], amp_chunk.buf.at[rows])):
            pltpu.make_async_copy(part, part, sem.at[i]).wait()

    def multiply(lam_rows, amp_rows):
        depth = lam_rows.shape[0]
        l = lam_rows[:, lanes(core)].T * jnp.concatenate([ab_col[...]] * (depth // 128), axis=1)
        l_hi = l.astype(BF16)
        l_lo = (l - l_hi.astype(F32)).astype(BF16)
        left[:, 0:depth] = l_hi
        left[:, depth : 2 * depth] = l_hi
        left[:, 2 * depth : 3 * depth] = l_lo
        a = amp_rows[...] * cd_row[0:1, :]
        a_hi = a.astype(BF16)
        a_lo = (a - a_hi.astype(F32)).astype(BF16)
        right[0:depth] = a_hi
        right[depth : 2 * depth] = a_lo
        right[2 * depth : 3 * depth] = a_hi
        mine = pl.ds(pl.multiple_of((HALF_LANES - HALF) * core, 64), HALF)
        out[...] += jnp.dot(left[mine, 0 : 3 * depth], right[0 : 3 * depth], preferred_element_type=F32)

    def on_kind(j, whole, half):
        pl.when((j >= 0) & (j < MAIN))(lambda: whole(j))
        pl.when((j >= MAIN) & (j < CHUNKS))(lambda: half(j - MAIN))

    def hand_over(j):
        def whole(j):
            for chunk in main(j):
                chunk.got(3, 3)
                chunk.got(4)
            for copy in share_main(j):
                copy.start()

        def half(j):
            for chunk in small(j):
                chunk.got(3, 3)
            for copy in share_early(j):
                copy.start()
            for chunk in small(j):
                chunk.got(4)
            for copy in share_far(j):
                copy.start()

        on_kind(j, whole, half)

    def add_product(j):
        def whole(j):
            for copy in share_main(j):
                copy.wait_recv()
            multiply(lam_main.at[j], amp_main.at[j])
            for chunk in main(j):
                chunk.sent()
            for copy in share_main(j):
                copy.wait_send()

        def half(j):
            small_wait(j, small_core_recv.at[j, 0], 7)
            small_wait(j, small_core_recv.at[j, 1], 1)
            multiply(lam_small.at[j], amp_small.at[j])

        on_kind(j, whole, half)

    def tick(t, _):
        on_chunk(t + 2, lambda chunk: chunk.cross_own())
        on_chunk(t + 1, lambda chunk: chunk.ring_own())
        on_chunk(t, lambda chunk: chunk.ring_partner())

        @pl.when(t < CHUNKS)
        def _():
            hand_over(t - 3)

        on_chunk(t, lambda chunk: chunk.pass_own())
        on_chunk(t - 1, lambda chunk: chunk.pass_partner())

        @pl.when(t == 0)
        def _():
            for chunk in last:
                chunk.pass_last()

        for step, at in enumerate(LAST_AT):

            @pl.when(t == at)
            def _(step=step):
                for chunk in last:
                    chunk.cross_last(step)

        @pl.when(t == LAST_SHARE)
        def _():
            for chunk in last:
                for step in range(4):
                    chunk.got(3 + step)
            for copy in share_last():
                copy.start()

        @pl.when(t == LAST_MULTIPLY)
        def _():
            for copy in share_last():
                copy.wait_recv()
            multiply(lam_last, amp_last)

        @pl.when(t == CHUNKS)
        def _():
            hand_over(t - 3)

        @pl.when(t >= CHUNKS)
        def _():
            hand_over(t - 2)

        add_product(t - 3)
        return 0

    lax.fori_loop(0, CHUNKS + 3, tick, 0)
    for j in range(SMALL):
        for chunk in small(j):
            chunk.sent()
        small_wait(j, small_core_send.at[j], 8)
    for chunk in last:
        chunk.sent()
    for copy in share_last():
        copy.wait_send()


def gather_multiply(lambdas, amplitudes, virt_irrep, ab_first, ab_second, cd_first, cd_second):
    dma = pltpu.SemaphoreType.DMA
    most = 3 * 2 * SOURCES * max(MAIN_ROWS, SMALL_ROWS, LAST_ROWS)
    rows = [virt_irrep, ab_first, ab_second, cd_first, cd_second]
    buffers = [
        pltpu.VMEM(shape, F32)
        for shape in (
            (MAIN, 2 * SOURCES * MAIN_ROWS, WIDTH),
            (SMALL, 2 * SOURCES * SMALL_ROWS, WIDTH),
            (2 * SOURCES * LAST_ROWS, WIDTH),
        )
        for _ in range(2)
    ]
    return pl.pallas_call(
        kernel,
        out_shape=pltpu.VMEM((HALF, WIDTH), F32),
        in_specs=[pl.BlockSpec(memory_space=pl.ANY)] * 7,
        out_specs=pl.BlockSpec(memory_space=pltpu.VMEM),
        scratch_shapes=[pltpu.VMEM(x.shape, I32) for x in rows]
        + buffers
        + [
            pltpu.VMEM((HALF_LANES, most), BF16),
            pltpu.VMEM((most, WIDTH), BF16),
            pltpu.VMEM((8, TABLE), F32),
            pltpu.VMEM((TABLE, 128), F32),
            pltpu.VMEM((8, HALF_LANES), F32),
            pltpu.VMEM((HALF_LANES, 128), F32),
            pltpu.VMEM((8, WIDTH), F32),
            dma((7,)),
            dma((2, MAIN)),
            dma((2, MAIN, 5)),
            dma((2, SMALL)),
            dma((2, SMALL, 5)),
            dma((2,)),
            dma((2, 7)),
            dma((MAIN, 2)),
            dma((MAIN, 2)),
            dma((SMALL, 2)),
            dma((SMALL, 2, 2)),
            dma((2,)),
            dma((2,)),
        ],
        compiler_params=pltpu.CompilerParams(collective_id=0, has_side_effects=True, vmem_limit_bytes=54 << 20),
        cost_estimate=pl.CostEstimate(flops=6 * 3200 * HALF * WIDTH, bytes_accessed=8 << 20, transcendentals=0),
    )(lambdas, amplitudes, *rows)


def solution(mesh):
    return jax.shard_map(
        gather_multiply,
        mesh=mesh,
        in_specs=(
            P(("col", "depth"), "row"),
            P(("row", "depth"), "col"),
            P(),
            P(("row", "depth")),
            P(("row", "depth")),
            P("col"),
            P("col"),
        ),
        out_specs=P(("row", "depth"), "col"),
        check_vma=False,
    )
```

```python
import functools

import jax
import jax.numpy as jnp
from jax import lax
from jax.experimental import pallas as pl
from jax.experimental.pallas import tpu as pltpu
from jax.sharding import PartitionSpec as P

MESH = pl.DeviceIdType.MESH
F32, BF16, I32 = jnp.float32, jnp.bfloat16, jnp.int32

MAIN, MAIN_ROWS = 11, 16
SMALL, SMALL_ROWS = 1, 8
CHUNKS = MAIN + SMALL
LAST_ROWS = 16
LAST_AT = (0, 2, 4, 7)
LAST_SHARE, LAST_MULTIPLY = 9, 10
SOURCES = 8
WIDTH = 1408
HALF = 704
HALF_LANES = 768
HALF_AT = 640
ORBITALS = 1200
TABLE = 1280


class Chunk:
    def __init__(self, side, buf, rows, start, send, recv):
        self.side, self.buf, self.rows, self.start, self.send, self.recv = side, buf, rows, start, send, recv

    def at(self, block):
        first = (self.side.core * SOURCES + block) * self.rows
        return self.buf.at[pl.ds(pl.multiple_of(first, 8), self.rows)]

    def own(self):
        return self.side.own.at[pl.ds(pl.multiple_of(self.start, 8), self.rows)]

    def lay(self, sem):
        pltpu.make_async_copy(self.own(), self.at(self.side.me), sem).start()

    def put(self, block, target, kind, own=False):
        here = self.at(block)
        pltpu.make_async_remote_copy(
            src_ref=self.own() if own else here,
            dst_ref=here,
            send_sem=self.send,
            recv_sem=self.recv(kind),
            device_id=self.side.device(target),
            device_id_type=MESH,
        ).start()

    def wait(self, sem, blocks):
        part = self.buf.at[pl.ds(0, blocks * self.rows)]
        pltpu.make_async_copy(part, part, sem).wait()

    def got(self, kind, blocks=1):
        self.wait(self.recv(kind), blocks)

    def sent(self):
        self.wait(self.send, 7)

    def cross_own(self):
        self.put(self.side.me, self.side.pair, 0, own=True)

    def ring_own(self):
        side = self.side
        self.put(side.me, side.ahead, 1, own=True)
        self.put(side.me, side.behind, 3, own=True)

    def ring_partner(self):
        side = self.side
        self.got(0)
        block = side.pair
        self.put(block, side.ahead, 2)
        self.put(block, side.behind, 3)

    def pass_own(self):
        side = self.side
        self.got(1)
        self.put(side.behind, side.ahead, 3)

    def pass_partner(self):
        side = self.side
        self.got(2)
        self.put(side.pair_behind, side.ahead, 4)

    def ring_last(self):
        side = self.side
        self.put(side.me, side.ahead, 0, own=True)
        self.put(side.me, side.behind, 1, own=True)

    def pass_last(self):
        side = self.side
        self.got(0)
        self.put(side.behind, side.ahead, 2)

    def cross_last(self, step):
        side = self.side
        if step >= 2:
            self.got(step - 1)
        block = (side.me, side.behind, side.ahead, side.opposite)[step]
        self.put(block, side.pair, 3 + step)


class Side:
    def __init__(self, own, core, me, ring, plane, device):
        self.own, self.core, self.me = own, core, me
        self.device = device
        way = 1 - 2 * core
        self.ahead, self.behind, self.opposite = ring(me, way), ring(me, -way), ring(me, 2)
        self.pair, self.pair_ahead, self.pair_behind = plane(me), plane(self.ahead), plane(self.behind)
        self.far = plane(self.opposite)


def set_signs(virt, first, second, row_out, table_col):
    tile = lax.broadcasted_iota(I32, (TABLE, 128), 0)
    full = first.shape[0]
    for at in range(0, full, 128):
        width = min(128, full - at)
        lanes = pl.ds(at, width)
        held = table_col[:, 0:width]
        rows = tile[:, 0:width]
        of_first = jnp.where(rows == first[lanes].reshape(1, width), held, 0.0)
        of_second = jnp.where(rows == second[lanes].reshape(1, width), held, 0.0)
        gap = jnp.sum(of_first - of_second, axis=0, keepdims=True)
        row_out[0:1, lanes] = jnp.where(gap > 0.0, -1.0, 1.0)


def kernel(
    lam, amp, virt_in, ab_first_in, ab_second_in, cd_first_in, cd_second_in, out,
    virt, ab_first, ab_second, cd_first, cd_second,
    lam_main, amp_main, lam_small, amp_small, lam_last, amp_last, left, right,
    table_row, table_col, ab_row, ab_col, cd_row,
    local_sem, main_send, main_recv, small_send, small_recv, last_send, last_recv,
    core_send, core_recv, small_core_send, small_core_recv, last_core_send, last_core_recv,
):
    row, col, core = lax.axis_index("row"), lax.axis_index("col"), lax.axis_index("depth")
    lam_side = Side(
        lam, core, col,
        lambda k, s: (k + 2 * s + 8) % 8,
        lambda k: k + 1 - 2 * (k % 2),
        lambda k: (row, k, core),
    )
    amp_side = Side(
        amp, core, row,
        lambda k, s: k // 4 * 4 + (k + s + 4) % 4,
        lambda k: (k + 4) % 8,
        lambda k: (k, col, core),
    )
    sides = (lam_side, amp_side)
    other = (row, col, 1 - core)

    barrier = pltpu.get_barrier_semaphore()
    partners = [other]
    for side in sides:
        partners += [side.device(k) for k in (side.pair, side.ahead, side.behind)]
    for partner in partners:
        pl.semaphore_signal(barrier, inc=1, device_id=partner, device_id_type=MESH)

    staged = [
        pltpu.make_async_copy(src, dst, local_sem.at[2 + i])
        for i, (src, dst) in enumerate(
            (
                (virt_in, virt),
                (ab_first_in, ab_first),
                (ab_second_in, ab_second),
                (cd_first_in, cd_first),
                (cd_second_in, cd_second),
            )
        )
    ]
    for copy in staged:
        copy.start()
    pl.semaphore_wait(barrier, len(partners))

    def main(j):
        return [
            Chunk(side, buf.at[j], MAIN_ROWS, j * MAIN_ROWS, main_send.at[i, j], lambda k, i=i: main_recv.at[i, j, k])
            for i, (side, buf) in enumerate(zip(sides, (lam_main, amp_main)))
        ]

    def small(j):
        start = MAIN * MAIN_ROWS + j * SMALL_ROWS
        return [
            Chunk(side, buf.at[j], SMALL_ROWS, start, small_send.at[i, j], lambda k, i=i: small_recv.at[i, j, k])
            for i, (side, buf) in enumerate(zip(sides, (lam_small, amp_small)))
        ]

    start = MAIN * MAIN_ROWS + SMALL * SMALL_ROWS
    last = [
        Chunk(side, buf, LAST_ROWS, start, last_send.at[i], lambda k, i=i: last_recv.at[i, k])
        for i, (side, buf) in enumerate(zip(sides, (lam_last, amp_last)))
    ]

    def on_chunk(j, do):
        @pl.when((j >= 0) & (j < MAIN))
        def _():
            for chunk in main(j):
                do(chunk)

        @pl.when((j >= MAIN) & (j < CHUNKS))
        def _():
            for chunk in small(j - MAIN):
                do(chunk)

    for chunk in main(0):
        chunk.cross_own()
    for chunk in main(0):
        chunk.ring_own()
    for chunk in last:
        chunk.ring_last()
    for chunk in main(1):
        chunk.cross_own()

    def lay(j, _):
        for i, chunk in enumerate(main(j)):
            chunk.lay(local_sem.at[i])
        return 0

    lax.fori_loop(0, MAIN, lay, 0)
    for j in range(SMALL):
        for i, chunk in enumerate(small(j)):
            chunk.lay(local_sem.at[i])
    for i, chunk in enumerate(last):
        chunk.lay(local_sem.at[i])
    for copy in staged:
        copy.wait()
    table_row[...] = jnp.zeros_like(table_row)
    table_row[0:1, 0:ORBITALS] = virt[...].astype(F32).reshape(1, ORBITALS)
    table_col[...] = jnp.broadcast_to(table_row[0:1, :], (128, TABLE)).T
    ab_row[...] = jnp.ones_like(ab_row)
    set_signs(virt, ab_first, ab_second, ab_row, table_col)
    set_signs(virt, cd_first, cd_second, cd_row, table_col)
    shifted = pltpu.roll(ab_row[...], (HALF_LANES - HALF) * core, 1)
    ab_col[...] = jnp.broadcast_to(shifted[0:1, :], (128, HALF_LANES)).T
    out[...] = jnp.zeros_like(out)
    for i, side in enumerate(sides):
        pltpu.make_async_copy(side.own, side.own, local_sem.at[i]).wait()

    def lanes(of):
        return pl.ds(pl.multiple_of(HALF_AT * of, 128), HALF_LANES)

    def to_core(parts, send, recv):
        return [
            pltpu.make_async_remote_copy(
                src_ref=part, dst_ref=part, send_sem=send.at[i], recv_sem=recv.at[i], device_id=other, device_id_type=MESH
            )
            for i, part in enumerate(parts)
        ]

    def share(chunks, send, recv):
        lam_chunk, amp_chunk = chunks
        rows = SOURCES * lam_chunk.rows
        mine = pl.ds(pl.multiple_of(core * rows, 64), rows)
        return to_core((lam_chunk.buf.at[mine, lanes(1 - core)], amp_chunk.buf.at[mine]), send, recv)

    def share_main(j):
        return share(main(j), core_send.at[j], core_recv.at[j])

    def share_last():
        return share(last, last_core_send, last_core_recv)

    def share_block(chunks, block_of, send, recv):
        lam_chunk, amp_chunk = chunks
        parts = (lam_chunk.at(block_of(lam_side)).at[:, lanes(1 - core)], amp_chunk.at(block_of(amp_side)))
        return to_core(parts, send, recv)

    def far(side):
        return side.far

    def share_early(j):
        copies = []
        for name in ("me", "ahead", "behind", "opposite", "pair", "pair_ahead", "pair_behind"):
            copies += share_block(small(j), lambda side, name=name: getattr(side, name), small_core_send.at[j], small_core_recv.at[j, 0])
        return copies

    def share_far(j):
        return share_block(small(j), far, small_core_send.at[j], small_core_recv.at[j, 1])

    def small_wait(j, sem, blocks):
        lam_chunk, amp_chunk = small(j)
        rows = pl.ds(0, blocks * SMALL_ROWS)
        for i, part in enumerate((lam_chunk.buf.at[rows, lanes(0)], amp_chunk.buf.at[rows])):
            pltpu.make_async_copy(part, part, sem.at[i]).wait()

    def multiply(lam_rows, amp_rows):
        depth = lam_rows.shape[0]
        l = lam_rows[:, lanes(core)].T * jnp.concatenate([ab_col[...]] * (depth // 128), axis=1)
        l_hi = l.astype(BF16)
        l_lo = (l - l_hi.astype(F32)).astype(BF16)
        left[:, 0:depth] = l_hi
        left[:, depth : 2 * depth] = l_hi
        left[:, 2 * depth : 3 * depth] = l_lo
        a = amp_rows[...] * cd_row[0:1, :]
        a_hi = a.astype(BF16)
        a_lo = (a - a_hi.astype(F32)).astype(BF16)
        right[0:depth] = a_hi
        right[depth : 2 * depth] = a_lo
        right[2 * depth : 3 * depth] = a_hi
        mine = pl.ds(pl.multiple_of((HALF_LANES - HALF) * core, 64), HALF)
        out[...] += jnp.dot(left[mine, 0 : 3 * depth], right[0 : 3 * depth], preferred_element_type=F32)

    def on_kind(j, whole, half):
        pl.when((j >= 0) & (j < MAIN))(lambda: whole(j))
        pl.when((j >= MAIN) & (j < CHUNKS))(lambda: half(j - MAIN))

    def hand_over(j):
        def whole(j):
            for chunk in main(j):
                chunk.got(3, 3)
                chunk.got(4)
            for copy in share_main(j):
                copy.start()

        def half(j):
            for chunk in small(j):
                chunk.got(3, 3)
            for copy in share_early(j):
                copy.start()
            for chunk in small(j):
                chunk.got(4)
            for copy in share_far(j):
                copy.start()

        on_kind(j, whole, half)

    def add_product(j):
        def whole(j):
            for copy in share_main(j):
                copy.wait_recv()
            multiply(lam_main.at[j], amp_main.at[j])
            for chunk in main(j):
                chunk.sent()
            for copy in share_main(j):
                copy.wait_send()

        def half(j):
            small_wait(j, small_core_recv.at[j, 0], 7)
            small_wait(j, small_core_recv.at[j, 1], 1)
            multiply(lam_small.at[j], amp_small.at[j])

        on_kind(j, whole, half)

    def tick(t, _):
        on_chunk(t + 2, lambda chunk: chunk.cross_own())
        on_chunk(t + 1, lambda chunk: chunk.ring_own())
        on_chunk(t, lambda chunk: chunk.ring_partner())

        @pl.when(t < CHUNKS)
        def _():
            hand_over(t - 3)

        on_chunk(t, lambda chunk: chunk.pass_own())
        on_chunk(t - 1, lambda chunk: chunk.pass_partner())

        @pl.when(t == 0)
        def _():
            for chunk in last:
                chunk.pass_last()

        for step, at in enumerate(LAST_AT):

            @pl.when(t == at)
            def _(step=step):
                for chunk in last:
                    chunk.cross_last(step)

        @pl.when(t == LAST_SHARE)
        def _():
            for chunk in last:
                for step in range(4):
                    chunk.got(3 + step)
            for copy in share_last():
                copy.start()

        @pl.when(t == LAST_MULTIPLY)
        def _():
            for copy in share_last():
                copy.wait_recv()
            multiply(lam_last, amp_last)

        @pl.when(t >= CHUNKS - 1)
        def _():
            hand_over(t - 2)

        add_product(t - 3)
        return 0

    lax.fori_loop(0, CHUNKS + 3, tick, 0)
    for j in range(SMALL):
        for chunk in small(j):
            chunk.sent()
        small_wait(j, small_core_send.at[j], 8)
    for chunk in last:
        chunk.sent()
    for copy in share_last():
        copy.wait_send()


def gather_multiply(lambdas, amplitudes, virt_irrep, ab_first, ab_second, cd_first, cd_second):
    dma = pltpu.SemaphoreType.DMA
    most = 3 * 2 * SOURCES * max(MAIN_ROWS, SMALL_ROWS, LAST_ROWS)
    rows = [virt_irrep, ab_first, ab_second, cd_first, cd_second]
    buffers = [
        pltpu.VMEM(shape, F32)
        for shape in (
            (MAIN, 2 * SOURCES * MAIN_ROWS, WIDTH),
            (SMALL, 2 * SOURCES * SMALL_ROWS, WIDTH),
            (2 * SOURCES * LAST_ROWS, WIDTH),
        )
        for _ in range(2)
    ]
    return pl.pallas_call(
        kernel,
        out_shape=pltpu.VMEM((HALF, WIDTH), F32),
        in_specs=[pl.BlockSpec(memory_space=pl.ANY)] * 7,
        out_specs=pl.BlockSpec(memory_space=pltpu.VMEM),
        scratch_shapes=[pltpu.VMEM(x.shape, I32) for x in rows]
        + buffers
        + [
            pltpu.VMEM((HALF_LANES, most), BF16),
            pltpu.VMEM((most, WIDTH), BF16),
            pltpu.VMEM((8, TABLE), F32),
            pltpu.VMEM((TABLE, 128), F32),
            pltpu.VMEM((8, HALF_LANES), F32),
            pltpu.VMEM((HALF_LANES, 128), F32),
            pltpu.VMEM((8, WIDTH), F32),
            dma((7,)),
            dma((2, MAIN)),
            dma((2, MAIN, 5)),
            dma((2, SMALL)),
            dma((2, SMALL, 5)),
            dma((2,)),
            dma((2, 7)),
            dma((MAIN, 2)),
            dma((MAIN, 2)),
            dma((SMALL, 2)),
            dma((SMALL, 2, 2)),
            dma((2,)),
            dma((2,)),
        ],
        compiler_params=pltpu.CompilerParams(collective_id=0, has_side_effects=True, vmem_limit_bytes=54 << 20),
        cost_estimate=pl.CostEstimate(flops=6 * 3200 * HALF * WIDTH, bytes_accessed=8 << 20, transcendentals=0),
    )(lambdas, amplitudes, *rows)


def solution(mesh):
    return jax.shard_map(
        gather_multiply,
        mesh=mesh,
        in_specs=(
            P(("col", "depth"), "row"),
            P(("row", "depth"), "col"),
            P(),
            P(("row", "depth")),
            P(("row", "depth")),
            P("col"),
            P("col"),
        ),
        out_specs=P(("row", "depth"), "col"),
        check_vma=False,
    )
```

```python
import functools

import jax
import jax.numpy as jnp
from jax import lax
from jax.experimental import pallas as pl
from jax.experimental.pallas import tpu as pltpu
from jax.sharding import PartitionSpec as P

MESH = pl.DeviceIdType.MESH
F32, BF16, I32 = jnp.float32, jnp.bfloat16, jnp.int32

MAIN, MAIN_ROWS = 11, 16
SMALL, SMALL_ROWS = 1, 8
CHUNKS = MAIN + SMALL
LAST_ROWS = 16
LAST_AT = (0, 2, 4, 6)
LAST_SHARE, LAST_MULTIPLY = 8, 9
SOURCES = 8
WIDTH = 1408
HALF = 704
HALF_LANES = 768
HALF_AT = 640
ORBITALS = 1200
TABLE = 1280


class Chunk:
    def __init__(self, side, buf, rows, start, send, recv):
        self.side, self.buf, self.rows, self.start, self.send, self.recv = side, buf, rows, start, send, recv

    def at(self, block):
        first = (self.side.core * SOURCES + block) * self.rows
        return self.buf.at[pl.ds(pl.multiple_of(first, 8), self.rows)]

    def own(self):
        return self.side.own.at[pl.ds(pl.multiple_of(self.start, 8), self.rows)]

    def lay(self, sem):
        pltpu.make_async_copy(self.own(), self.at(self.side.me), sem).start()

    def put(self, block, target, kind, own=False):
        here = self.at(block)
        pltpu.make_async_remote_copy(
            src_ref=self.own() if own else here,
            dst_ref=here,
            send_sem=self.send,
            recv_sem=self.recv(kind),
            device_id=self.side.device(target),
            device_id_type=MESH,
        ).start()

    def wait(self, sem, blocks):
        part = self.buf.at[pl.ds(0, blocks * self.rows)]
        pltpu.make_async_copy(part, part, sem).wait()

    def got(self, kind, blocks=1):
        self.wait(self.recv(kind), blocks)

    def sent(self):
        self.wait(self.send, 7)

    def cross_own(self):
        self.put(self.side.me, self.side.pair, 0, own=True)

    def ring_own(self):
        side = self.side
        self.put(side.me, side.ahead, 1, own=True)
        self.put(side.me, side.behind, 3, own=True)

    def ring_partner(self):
        side = self.side
        self.got(0)
        block = side.pair
        self.put(block, side.ahead, 2)
        self.put(block, side.behind, 3)

    def pass_own(self):
        side = self.side
        self.got(1)
        self.put(side.behind, side.ahead, 3)

    def pass_partner(self):
        side = self.side
        self.got(2)
        self.put(side.pair_behind, side.ahead, 4)

    def ring_last(self):
        side = self.side
        self.put(side.me, side.ahead, 0, own=True)
        self.put(side.me, side.behind, 1, own=True)

    def pass_last(self):
        side = self.side
        self.got(0)
        self.put(side.behind, side.ahead, 2)

    def cross_last(self, step):
        side = self.side
        if step >= 2:
            self.got(step - 1)
        block = (side.me, side.behind, side.ahead, side.opposite)[step]
        self.put(block, side.pair, 3 + step)


class Side:
    def __init__(self, own, core, me, ring, plane, device):
        self.own, self.core, self.me = own, core, me
        self.device = device
        way = 1 - 2 * core
        self.ahead, self.behind, self.opposite = ring(me, way), ring(me, -way), ring(me, 2)
        self.pair, self.pair_ahead, self.pair_behind = plane(me), plane(self.ahead), plane(self.behind)
        self.far = plane(self.opposite)


def set_signs(virt, first, second, row_out, table_col):
    tile = lax.broadcasted_iota(I32, (TABLE, 128), 0)
    full = first.shape[0]
    for at in range(0, full, 128):
        width = min(128, full - at)
        lanes = pl.ds(at, width)
        held = table_col[:, 0:width]
        rows = tile[:, 0:width]
        of_first = jnp.where(rows == first[lanes].reshape(1, width), held, 0.0)
        of_second = jnp.where(rows == second[lanes].reshape(1, width), held, 0.0)
        gap = jnp.sum(of_first - of_second, axis=0, keepdims=True)
        row_out[0:1, lanes] = jnp.where(gap > 0.0, -1.0, 1.0)


def kernel(
    lam, amp, virt_in, ab_first_in, ab_second_in, cd_first_in, cd_second_in, out,
    virt, ab_first, ab_second, cd_first, cd_second,
    lam_main, amp_main, lam_small, amp_small, lam_last, amp_last, left, right,
    table_row, table_col, ab_row, ab_col, cd_row,
    local_sem, main_send, main_recv, small_send, small_recv, last_send, last_recv,
    core_send, core_recv, small_core_send, small_core_recv, last_core_send, last_core_recv,
):
    row, col, core = lax.axis_index("row"), lax.axis_index("col"), lax.axis_index("depth")
    lam_side = Side(
        lam, core, col,
        lambda k, s: (k + 2 * s + 8) % 8,
        lambda k: k + 1 - 2 * (k % 2),
        lambda k: (row, k, core),
    )
    amp_side = Side(
        amp, core, row,
        lambda k, s: k // 4 * 4 + (k + s + 4) % 4,
        lambda k: (k + 4) % 8,
        lambda k: (k, col, core),
    )
    sides = (lam_side, amp_side)
    other = (row, col, 1 - core)

    barrier = pltpu.get_barrier_semaphore()
    partners = [other]
    for side in sides:
        partners += [side.device(k) for k in (side.pair, side.ahead, side.behind)]
    for partner in partners:
        pl.semaphore_signal(barrier, inc=1, device_id=partner, device_id_type=MESH)

    staged = [
        pltpu.make_async_copy(src, dst, local_sem.at[2 + i])
        for i, (src, dst) in enumerate(
            (
                (virt_in, virt),
                (ab_first_in, ab_first),
                (ab_second_in, ab_second),
                (cd_first_in, cd_first),
                (cd_second_in, cd_second),
            )
        )
    ]
    for copy in staged:
        copy.start()
    pl.semaphore_wait(barrier, len(partners))

    def main(j):
        return [
            Chunk(side, buf.at[j], MAIN_ROWS, j * MAIN_ROWS, main_send.at[i, j], lambda k, i=i: main_recv.at[i, j, k])
            for i, (side, buf) in enumerate(zip(sides, (lam_main, amp_main)))
        ]

    def small(j):
        start = MAIN * MAIN_ROWS + j * SMALL_ROWS
        return [
            Chunk(side, buf.at[j], SMALL_ROWS, start, small_send.at[i, j], lambda k, i=i: small_recv.at[i, j, k])
            for i, (side, buf) in enumerate(zip(sides, (lam_small, amp_small)))
        ]

    start = MAIN * MAIN_ROWS + SMALL * SMALL_ROWS
    last = [
        Chunk(side, buf, LAST_ROWS, start, last_send.at[i], lambda k, i=i: last_recv.at[i, k])
        for i, (side, buf) in enumerate(zip(sides, (lam_last, amp_last)))
    ]

    def on_chunk(j, do):
        @pl.when((j >= 0) & (j < MAIN))
        def _():
            for chunk in main(j):
                do(chunk)

        @pl.when((j >= MAIN) & (j < CHUNKS))
        def _():
            for chunk in small(j - MAIN):
                do(chunk)

    for chunk in main(0):
        chunk.cross_own()
    for chunk in main(0):
        chunk.ring_own()
    for chunk in last:
        chunk.ring_last()
    for chunk in main(1):
        chunk.cross_own()

    def lay(j, _):
        for i, chunk in enumerate(main(j)):
            chunk.lay(local_sem.at[i])
        return 0

    lax.fori_loop(0, MAIN, lay, 0)
    for j in range(SMALL):
        for i, chunk in enumerate(small(j)):
            chunk.lay(local_sem.at[i])
    for i, chunk in enumerate(last):
        chunk.lay(local_sem.at[i])
    for copy in staged:
        copy.wait()
    table_row[...] = jnp.zeros_like(table_row)
    table_row[0:1, 0:ORBITALS] = virt[...].astype(F32).reshape(1, ORBITALS)
    table_col[...] = jnp.broadcast_to(table_row[0:1, :], (128, TABLE)).T
    ab_row[...] = jnp.ones_like(ab_row)
    set_signs(virt, ab_first, ab_second, ab_row, table_col)
    set_signs(virt, cd_first, cd_second, cd_row, table_col)
    shifted = pltpu.roll(ab_row[...], (HALF_LANES - HALF) * core, 1)
    ab_col[...] = jnp.broadcast_to(shifted[0:1, :], (128, HALF_LANES)).T
    out[...] = jnp.zeros_like(out)
    for i, side in enumerate(sides):
        pltpu.make_async_copy(side.own, side.own, local_sem.at[i]).wait()

    def lanes(of):
        return pl.ds(pl.multiple_of(HALF_AT * of, 128), HALF_LANES)

    def to_core(parts, send, recv):
        return [
            pltpu.make_async_remote_copy(
                src_ref=part, dst_ref=part, send_sem=send.at[i], recv_sem=recv.at[i], device_id=other, device_id_type=MESH
            )
            for i, part in enumerate(parts)
        ]

    def share(chunks, send, recv):
        lam_chunk, amp_chunk = chunks
        rows = SOURCES * lam_chunk.rows
        mine = pl.ds(pl.multiple_of(core * rows, 64), rows)
        return to_core((lam_chunk.buf.at[mine, lanes(1 - core)], amp_chunk.buf.at[mine]), send, recv)

    def share_main(j):
        return share(main(j), core_send.at[j], core_recv.at[j])

    def share_last():
        return share(last, last_core_send, last_core_recv)

    def share_block(chunks, block_of, send, recv):
        lam_chunk, amp_chunk = chunks
        parts = (lam_chunk.at(block_of(lam_side)).at[:, lanes(1 - core)], amp_chunk.at(block_of(amp_side)))
        return to_core(parts, send, recv)

    def far(side):
        return side.far

    def share_early(j):
        copies = []
        for name in ("me", "ahead", "behind", "opposite", "pair", "pair_ahead", "pair_behind"):
            copies += share_block(small(j), lambda side, name=name: getattr(side, name), small_core_send.at[j], small_core_recv.at[j, 0])
        return copies

    def share_far(j):
        return share_block(small(j), far, small_core_send.at[j], small_core_recv.at[j, 1])

    def small_wait(j, sem, blocks):
        lam_chunk, amp_chunk = small(j)
        rows = pl.ds(0, blocks * SMALL_ROWS)
        for i, part in enumerate((lam_chunk.buf.at[rows, lanes(0)], amp_chunk.buf.at[rows])):
            pltpu.make_async_copy(part, part, sem.at[i]).wait()

    def multiply(lam_rows, amp_rows):
        depth = lam_rows.shape[0]
        l = lam_rows[:, lanes(core)].T * jnp.concatenate([ab_col[...]] * (depth // 128), axis=1)
        l_hi = l.astype(BF16)
        l_lo = (l - l_hi.astype(F32)).astype(BF16)
        left[:, 0:depth] = l_hi
        left[:, depth : 2 * depth] = l_hi
        left[:, 2 * depth : 3 * depth] = l_lo
        a = amp_rows[...] * cd_row[0:1, :]
        a_hi = a.astype(BF16)
        a_lo = (a - a_hi.astype(F32)).astype(BF16)
        right[0:depth] = a_hi
        right[depth : 2 * depth] = a_lo
        right[2 * depth : 3 * depth] = a_hi
        mine = pl.ds(pl.multiple_of((HALF_LANES - HALF) * core, 64), HALF)
        out[...] += jnp.dot(left[mine, 0 : 3 * depth], right[0 : 3 * depth], preferred_element_type=F32)

    def on_kind(j, whole, half):
        pl.when((j >= 0) & (j < MAIN))(lambda: whole(j))
        pl.when((j >= MAIN) & (j < CHUNKS))(lambda: half(j - MAIN))

    def hand_over(j):
        def whole(j):
            for chunk in main(j):
                chunk.got(3, 3)
                chunk.got(4)
            for copy in share_main(j):
                copy.start()

        def half(j):
            for chunk in small(j):
                chunk.got(3, 3)
            for copy in share_early(j):
                copy.start()
            for chunk in small(j):
                chunk.got(4)
            for copy in share_far(j):
                copy.start()

        on_kind(j, whole, half)

    def add_product(j):
        def whole(j):
            for copy in share_main(j):
                copy.wait_recv()
            multiply(lam_main.at[j], amp_main.at[j])
            for chunk in main(j):
                chunk.sent()
            for copy in share_main(j):
                copy.wait_send()

        def half(j):
            small_wait(j, small_core_recv.at[j, 0], 7)
            small_wait(j, small_core_recv.at[j, 1], 1)
            multiply(lam_small.at[j], amp_small.at[j])

        on_kind(j, whole, half)

    def tick(t, _):
        on_chunk(t + 2, lambda chunk: chunk.cross_own())
        on_chunk(t + 1, lambda chunk: chunk.ring_own())
        on_chunk(t, lambda chunk: chunk.ring_partner())

        @pl.when(t < CHUNKS)
        def _():
            hand_over(t - 3)

        on_chunk(t, lambda chunk: chunk.pass_own())
        on_chunk(t - 1, lambda chunk: chunk.pass_partner())

        @pl.when(t == 0)
        def _():
            for chunk in last:
                chunk.pass_last()

        for step, at in enumerate(LAST_AT):

            @pl.when(t == at)
            def _(step=step):
                for chunk in last:
                    chunk.cross_last(step)

        @pl.when(t == LAST_SHARE)
        def _():
            for chunk in last:
                for step in range(4):
                    chunk.got(3 + step)
            for copy in share_last():
                copy.start()

        @pl.when(t == LAST_MULTIPLY)
        def _():
            for copy in share_last():
                copy.wait_recv()
            multiply(lam_last, amp_last)

        @pl.when(t >= CHUNKS - 1)
        def _():
            hand_over(t - 2)

        add_product(t - 3)
        return 0

    lax.fori_loop(0, CHUNKS + 3, tick, 0)
    for j in range(SMALL):
        for chunk in small(j):
            chunk.sent()
        small_wait(j, small_core_send.at[j], 8)
    for chunk in last:
        chunk.sent()
    for copy in share_last():
        copy.wait_send()


def gather_multiply(lambdas, amplitudes, virt_irrep, ab_first, ab_second, cd_first, cd_second):
    dma = pltpu.SemaphoreType.DMA
    most = 3 * 2 * SOURCES * max(MAIN_ROWS, SMALL_ROWS, LAST_ROWS)
    rows = [virt_irrep, ab_first, ab_second, cd_first, cd_second]
    buffers = [
        pltpu.VMEM(shape, F32)
        for shape in (
            (MAIN, 2 * SOURCES * MAIN_ROWS, WIDTH),
            (SMALL, 2 * SOURCES * SMALL_ROWS, WIDTH),
            (2 * SOURCES * LAST_ROWS, WIDTH),
        )
        for _ in range(2)
    ]
    return pl.pallas_call(
        kernel,
        out_shape=pltpu.VMEM((HALF, WIDTH), F32),
        in_specs=[pl.BlockSpec(memory_space=pl.ANY)] * 7,
        out_specs=pl.BlockSpec(memory_space=pltpu.VMEM),
        scratch_shapes=[pltpu.VMEM(x.shape, I32) for x in rows]
        + buffers
        + [
            pltpu.VMEM((HALF_LANES, most), BF16),
            pltpu.VMEM((most, WIDTH), BF16),
            pltpu.VMEM((8, TABLE), F32),
            pltpu.VMEM((TABLE, 128), F32),
            pltpu.VMEM((8, HALF_LANES), F32),
            pltpu.VMEM((HALF_LANES, 128), F32),
            pltpu.VMEM((8, WIDTH), F32),
            dma((7,)),
            dma((2, MAIN)),
            dma((2, MAIN, 5)),
            dma((2, SMALL)),
            dma((2, SMALL, 5)),
            dma((2,)),
            dma((2, 7)),
            dma((MAIN, 2)),
            dma((MAIN, 2)),
            dma((SMALL, 2)),
            dma((SMALL, 2, 2)),
            dma((2,)),
            dma((2,)),
        ],
        compiler_params=pltpu.CompilerParams(collective_id=0, has_side_effects=True, vmem_limit_bytes=54 << 20),
        cost_estimate=pl.CostEstimate(flops=6 * 3200 * HALF * WIDTH, bytes_accessed=8 << 20, transcendentals=0),
    )(lambdas, amplitudes, *rows)


def solution(mesh):
    return jax.shard_map(
        gather_multiply,
        mesh=mesh,
        in_specs=(
            P(("col", "depth"), "row"),
            P(("row", "depth"), "col"),
            P(),
            P(("row", "depth")),
            P(("row", "depth")),
            P("col"),
            P("col"),
        ),
        out_specs=P(("row", "depth"), "col"),
        check_vma=False,
    )
```
